256 devices in a mesh: expert: 32 (over z, x_hi, core), mp: 8 (over x_lo, y).
Axes of the slice: x: 4 (x_hi: 2, x_lo: 2; x = x_hi * 2 + x_lo), y: 4, z: 8, core: 2. Of those that a mesh axis runs over, the one named last changes fastest.
Arguments:
- tokens: bfloat16 [1024, 5120], P('expert', 'mp'), may hold values from -6 to 6
- grad_out: bfloat16 [1024, 5120], P('expert', 'mp'), may hold values from -6 to 6
- expert_ids: int32 [1024, 2], P('expert'), may hold values from 0 to 3, as said below
- slot_ids: int32 [1024, 2], P('expert'), may hold values from -1 to 19, as said below
- gate_weights: bfloat16 [1024, 2], P('expert'), may hold values from 0.19921875 to 1
- gate_proj: bfloat16 [32, 1280, 5120], P('expert', 'mp'), may hold values from -0.078125 to 0.078125
- up_proj: bfloat16 [32, 1280, 5120], P('expert', 'mp'), may hold values from -0.078125 to 0.078125
- down_proj: bfloat16 [32, 1280, 5120], P('expert', 'mp'), may hold values from -0.0625 to 0.0625
Outputs:
- grad_tokens: bfloat16 [1024, 5120], P('expert', 'mp')
- grad_gates: float32 [1024, 2], P('expert')
- grad_gate_proj: bfloat16 [32, 1280, 5120], P('expert', 'mp')
- grad_up_proj: bfloat16 [32, 1280, 5120], P('expert', 'mp')
- grad_down_proj: bfloat16 [32, 1280, 5120], P('expert', 'mp')
The draws below stay inside these ranges and needn't reach their ends.
Inputs may be any that keep to these rules, and one draw needn't show every extreme that they name: `expert_ids`: the two experts of a token differ. `slot_ids`: within one group of 32 tokens, first choices in token order come before second choices; each choice takes the next free slot of its expert, and -1 marks one that finds all 20 slots taken. Live slots of one group and expert are distinct; in every group some expert has all 20 slots taken.
All inputs are finite; a program needn't handle non-finite values.
Results may differ from the reference program's by a relative error of at most 0.02.
Values may be sent and summed in bfloat16 or wider, within the bound.
No kernel may reach another device: no remote copies, remote signals or barrier semaphores. Data moves between devices by JAX's collectives and lax.ppermute only.
A program may use at most 128 MiB of HBM per device.

```python
import jax
import jax.numpy as jnp
from jax import lax

D = 5120
FF = 10240
SUB = 8
TOK_DEV = 32
EXPERTS = 4
SLICES = 32
FF_SUB = 1280
FF_DEV = 160
TOKENS = 1024
CAP = 20
ROWS = 640
N_MP = 8


def shuffle_one(subkey):
    return jax.random.permutation(subkey, TOK_DEV)


def routing(key):
    group_count = TOKENS // TOK_DEV
    hot_key, chosen_key, uniform_key, offset_key = jax.random.split(key, 4)
    hot_expert = jax.random.randint(hot_key, (group_count, 1), 0, EXPERTS, dtype=jnp.int32)
    shuffled = jax.vmap(shuffle_one)(jax.random.split(chosen_key, group_count))
    chosen = shuffled < CAP
    uniform_pick = jax.random.randint(uniform_key, (group_count, TOK_DEV), 0, EXPERTS, dtype=jnp.int32)
    first_choice = jnp.where(chosen, hot_expert, uniform_pick).astype(jnp.int32)
    offset = jax.random.randint(offset_key, (group_count, TOK_DEV), 1, EXPERTS, dtype=jnp.int32)
    second_choice = (first_choice + offset) % EXPERTS
    all_choices = jnp.concatenate([first_choice, second_choice], axis=1)
    onehot = (all_choices[..., None] == jnp.arange(EXPERTS, dtype=jnp.int32)[None, None, :]).astype(jnp.int32)
    earlier = jnp.sum((jnp.cumsum(onehot, axis=1) - onehot) * onehot, axis=2)
    slot_flat = jnp.where(earlier < CAP, earlier, -1).astype(jnp.int32)
    routes = jnp.stack([first_choice, second_choice], axis=-1).reshape(TOKENS, 2)
    slot_ids = jnp.stack([slot_flat[:, :TOK_DEV], slot_flat[:, TOK_DEV:]], axis=-1).reshape(TOKENS, 2)
    return (routes, slot_ids)


def draw_expert_ids(key, part):
    routes, slot_ids = routing(key)
    return routes


def draw_slot_ids(key, part):
    routes, slot_ids = routing(key)
    return slot_ids


def steps_of(key, extent, shards, smallest, largest):
    level = 1.0
    for axis_at, shards_of in shards:
        heights = jax.random.uniform(jax.random.fold_in(jax.random.fold_in(key, 6), axis_at), (shards_of,), jnp.float32, smallest / len(shards), largest / len(shards))
        level = level * jnp.repeat(jnp.exp(heights), extent[axis_at] // shards_of).reshape((-1,) + (1,) * (len(extent) - 1 - axis_at))
    return level


def scatter_about(own_key, dims, width, limit, shards=(), kind=jnp.bfloat16):
    result = width * jax.random.normal(own_key, dims, jnp.float32)
    if shards:
        result = result * steps_of(own_key, dims, shards, -0.22, 0.18)
    return jnp.clip(result, -limit, limit).astype(kind)


def setup_inputs(seed: int = 0) -> dict:
    streams_of = jax.random.split(jax.random.key(seed), 9)
    tokens = scatter_about(streams_of[0], (TOKENS, D), 1.0, 6.0, ((0, 32), (1, 8)))
    grad_out = scatter_about(streams_of[1], (TOKENS, D), 1.0, 6.0, ((0, 32), (1, 8)))
    expert_ids = draw_expert_ids(jax.random.fold_in(streams_of[8], 71), 0)
    slot_ids = draw_slot_ids(jax.random.fold_in(streams_of[8], 71), 0)
    gate_weights = jnp.clip(0.19921875 + 0.80078125 * jax.random.uniform(streams_of[4], (TOKENS, 2), jnp.float32) ** steps_of(streams_of[4], (TOKENS, 2), ((0, 32),), -0.2, 0.2), 0.19921875, 1.0).astype(jnp.bfloat16)
    gate_proj = scatter_about(streams_of[5], (SLICES, FF_SUB, D), D ** -0.5, 0.078125, ((0, 32), (1, 8)))
    up_proj = scatter_about(streams_of[6], (SLICES, FF_SUB, D), D ** -0.5, 0.078125, ((0, 32), (1, 8)))
    down_proj = scatter_about(streams_of[7], (SLICES, FF_SUB, D), FF ** -0.5, 0.0625, ((0, 32), (1, 8)))
    return {"tokens": tokens, "grad_out": grad_out, "expert_ids": expert_ids, "slot_ids": slot_ids, "gate_weights": gate_weights, "gate_proj": gate_proj, "up_proj": up_proj, "down_proj": down_proj}


SQRT_TWO_PI = 0.7978845608028654
CUBIC = 0.044715


def gelu_value(values):
    return 0.5 * values * (1.0 + jnp.tanh(SQRT_TWO_PI * (values + CUBIC * values * values * values)))


def gelu_slope(values):
    tanh_part = jnp.tanh(SQRT_TWO_PI * (values + CUBIC * values * values * values))
    return 0.5 * (1.0 + tanh_part) + 0.5 * values * (1.0 - tanh_part * tanh_part) * SQRT_TWO_PI * (1.0 + 3.0 * CUBIC * values * values)


def reference(tokens, grad_out, expert_ids, slot_ids, gate_weights, gate_proj, up_proj, down_proj):
    group_count = TOKENS // TOK_DEV
    group_of = jnp.arange(TOKENS, dtype=jnp.int32) // TOK_DEV
    is_live = slot_ids >= 0
    dump_index = group_count * EXPERTS * CAP
    where_to = (group_of[:, None] * EXPERTS + expert_ids) * CAP + slot_ids
    where_to = jnp.where(is_live, where_to, dump_index).astype(jnp.int32).reshape(-1)
    token_index = jnp.broadcast_to(jnp.arange(TOKENS, dtype=jnp.int32)[:, None], (TOKENS, 2)).reshape(-1)
    slot_table = jnp.full((dump_index + 1,), -1, jnp.int32).at[where_to].set(token_index)[:-1]
    gate_table = jnp.zeros((dump_index + 1,), jnp.bfloat16).at[where_to].set(gate_weights.reshape(-1))[:-1]
    slot_table = slot_table.reshape(group_count, EXPERTS, CAP).transpose(1, 0, 2).reshape(EXPERTS, ROWS)
    gate_table = gate_table.reshape(group_count, EXPERTS, CAP).transpose(1, 0, 2).reshape(EXPERTS, ROWS)
    full_gate = gate_proj.reshape(EXPERTS, FF, D).transpose(0, 2, 1)
    full_up = up_proj.reshape(EXPERTS, FF, D).transpose(0, 2, 1)
    full_down = down_proj.reshape(EXPERTS, FF, D)

    def one_expert(operands):
        slot_rows, row_gate, w_gate, w_up, w_down = operands
        has_token = (slot_rows >= 0)[:, None]
        safe_index = jnp.maximum(slot_rows, 0).astype(jnp.int32)
        inputs = jnp.where(has_token, tokens[safe_index], jnp.zeros((), jnp.bfloat16))
        upstream = jnp.where(has_token, grad_out[safe_index], jnp.zeros((), jnp.bfloat16))
        pre_gate = jnp.dot(inputs, w_gate, preferred_element_type=jnp.float32)
        pre_up = jnp.dot(inputs, w_up, preferred_element_type=jnp.float32)
        hidden = (gelu_value(pre_gate) * pre_up).astype(jnp.bfloat16)
        scaled = (row_gate.astype(jnp.float32)[:, None] * upstream.astype(jnp.float32)).astype(jnp.bfloat16)
        back_raw = jnp.dot(upstream, w_down.T, preferred_element_type=jnp.float32)
        back_grad = jnp.dot(scaled, w_down.T, preferred_element_type=jnp.float32)
        grad_down = jnp.dot(hidden.T, scaled, preferred_element_type=jnp.float32).astype(jnp.bfloat16)
        d_gate_pre = (back_grad * pre_up * gelu_slope(pre_gate)).astype(jnp.bfloat16)
        d_up_pre = (back_grad * gelu_value(pre_gate)).astype(jnp.bfloat16)
        grad_gate = jnp.dot(d_gate_pre.T, inputs, preferred_element_type=jnp.float32).astype(jnp.bfloat16)
        grad_up = jnp.dot(d_up_pre.T, inputs, preferred_element_type=jnp.float32).astype(jnp.bfloat16)
        row_total = jnp.zeros((ROWS, D), jnp.float32)
        score_total = jnp.zeros((ROWS,), jnp.float32)
        for piece in range(SUB):
            slice_total = jnp.zeros((ROWS, D), jnp.float32)
            for block in range(N_MP):
                lower = (piece * N_MP + block) * FF_DEV
                upper = lower + FF_DEV
                partial_value = jnp.dot(d_gate_pre[:, lower:upper], w_gate[:, lower:upper].T, preferred_element_type=jnp.float32)
                partial_value = partial_value + jnp.dot(d_up_pre[:, lower:upper], w_up[:, lower:upper].T, preferred_element_type=jnp.float32)
                partial_value = lax.optimization_barrier(partial_value.astype(jnp.bfloat16))
                slice_total = slice_total + partial_value.astype(jnp.float32)
            slice_round = lax.optimization_barrier(slice_total.astype(jnp.bfloat16))
            row_total = row_total + slice_round.astype(jnp.float32)
            lower = piece * FF_SUB
            upper = lower + FF_SUB
            scores = jnp.sum(hidden[:, lower:upper].astype(jnp.float32) * back_raw[:, lower:upper], axis=1)
            scores = lax.optimization_barrier(scores.astype(jnp.bfloat16))
            score_total = score_total + scores.astype(jnp.float32)
        grad_gate = grad_gate.reshape(SUB, FF_SUB, D)
        grad_up = grad_up.reshape(SUB, FF_SUB, D)
        grad_down = grad_down.reshape(SUB, FF_SUB, D)
        return row_total, score_total, grad_gate, grad_up, grad_down

    row_grad, row_score, grad_gate_proj, grad_up_proj, grad_down_proj = lax.map(
        one_expert, (slot_table, gate_table, full_gate, full_up, full_down))
    grad_gate_proj = grad_gate_proj.reshape(EXPERTS * SUB, FF_SUB, D)
    grad_up_proj = grad_up_proj.reshape(EXPERTS * SUB, FF_SUB, D)
    grad_down_proj = grad_down_proj.reshape(EXPERTS * SUB, FF_SUB, D)
    row_pick = jnp.clip(group_of[:, None] * CAP + slot_ids, 0, ROWS - 1).astype(jnp.int32)
    picked = row_grad[expert_ids, row_pick]
    grad_tokens = jnp.sum(jnp.where(is_live[..., None], picked, jnp.float32(0.0)), axis=1).astype(jnp.bfloat16)
    grad_gates = jnp.where(is_live, row_score[expert_ids, row_pick], jnp.float32(0.0))
    return grad_tokens, grad_gates, grad_gate_proj, grad_up_proj, grad_down_proj
```

```python
import functools

import jax
import jax.numpy as jnp
from jax import lax
from jax.experimental import pallas as pl
from jax.experimental.pallas import tpu as pltpu
from jax.sharding import Mesh
from jax.sharding import PartitionSpec as P

SQRT_TWO_PI = 0.7978845608028654
CUBIC = 0.044715

EXPERTS = 4
CAP = 20
TOK = 32
SHARE = 640
WIDTH = 5120
HID = 160
BLOCK = EXPERTS * CAP
ROWS = 8 * BLOCK
XAXES = ("xh", "xl")
VMEM_LIMIT = 56 * 1024 * 1024

BF16 = jnp.bfloat16
F32 = jnp.float32

OFFSET = (0, 1, -1, 2)


def fetch(value, axis, offset, size):
    return lax.ppermute(value, axis, [((i + offset) % size, i) for i in range(size)])


def add(*terms):
    total = terms[0].astype(F32)
    for term in terms[1:]:
        total = total + term.astype(F32)
    return total.astype(BF16)


def targets_of(pos_ref, eid_ref, sid_ref):
    relative = (eid_ref[...] - pos_ref[0] + EXPERTS) % EXPERTS
    return jnp.where(sid_ref[...] >= 0, relative * CAP + sid_ref[...], -1)


def pack_kernel(pos_ref, eid_ref, sid_ref, gate_ref, tok_ref, up_ref, *outs):
    target = targets_of(pos_ref, eid_ref, sid_ref)
    gate = gate_ref[...].astype(F32)
    lane = lax.broadcasted_iota(jnp.int32, (TOK, CAP), 1)
    over_tokens = (((0,), (0,)), ((), ()))
    for k in range(EXPERTS):
        first = target[:, 0:1] == lane + k * CAP
        second = target[:, 1:2] == lane + k * CAP
        one = jnp.where(first, 1.0, jnp.where(second, 1.0, 0.0)).astype(BF16)
        scale = jnp.where(
            first, gate[:, 0:1], jnp.where(second, gate[:, 1:2], 0.0)
        ).astype(BF16)
        outs[k][0] = lax.dot_general(
            one, tok_ref[...], over_tokens, preferred_element_type=F32
        ).astype(BF16)
        outs[k][1] = lax.dot_general(
            scale, up_ref[...], over_tokens, preferred_element_type=F32
        ).astype(BF16)


def combine_kernel(pos_ref, eid_ref, sid_ref, gate_ref, s0, s1, s2, s3, r0, r1, r2, r3, tok_ref, gates_ref):
    target = targets_of(pos_ref, eid_ref, sid_ref)
    gate = gate_ref[...].astype(F32)
    lane = lax.broadcasted_iota(jnp.int32, (TOK, CAP), 1)
    total = jnp.zeros((TOK, SHARE), F32)
    score = [jnp.zeros((TOK, 1), F32), jnp.zeros((TOK, 1), F32)]
    for k, (s_ref, r_ref) in enumerate(zip((s0, s1, s2, s3), (r0, r1, r2, r3))):
        hits = [target[:, c : c + 1] == lane + k * CAP for c in range(2)]
        one = jnp.where(hits[0], 1.0, jnp.where(hits[1], 1.0, 0.0)).astype(BF16)
        total = total + jnp.dot(one, r_ref[...], preferred_element_type=F32)
        for c in range(2):
            score[c] = score[c] + jnp.sum(
                jnp.where(hits[c], s_ref[...], 0.0), axis=1, keepdims=True
            )
    tok_ref[...] = total.astype(BF16)
    for c in range(2):
        gates_ref[:, c : c + 1] = score[c] / gate[:, c : c + 1]


def load_rows(pos_ref, pieces, by_x_first, slots, sems):
    xl = pos_ref[1]
    for core in range(2):
        own, nxt, prev, half0, half1 = pieces[5 * core : 5 * core + 5]
        for last in range(4):
            for inner in range(4):
                if last < 3:
                    source = (own, nxt, prev)[last].at[inner]
                else:
                    source = (half0, half1)[inner // 2].at[inner % 2]
                ix, iy = (inner, last) if by_x_first else (last, inner)
                parity = 1 if ix in (1, 2) else 0
                x_half = {0: 0, 1: xl, 2: 1 - xl, 3: 1}[ix]
                row = (x_half * 2 + core) * 2 * BLOCK
                if not isinstance(row, int):
                    row = pl.multiple_of(row, 2 * BLOCK)
                j = parity * 4 + iy
                pltpu.make_async_copy(
                    source, slots.at[j, pl.ds(row, 2 * BLOCK)], sems.at[j]
                ).start()


def await_slot(slots, sems, j):
    pltpu.make_async_copy(slots.at[j], slots.at[j], sems.at[j]).wait()


def column_of(pos_ref, j):
    xl, y = pos_ref[1], pos_ref[2]
    parity, iy = j // 4, j % 4
    offset = jnp.where(iy == 1, 1, jnp.where(iy == 2, 3, jnp.where(iy == 3, 2, 0)))
    block = ((xl + parity) % 2) * 4 + (y + offset) % 4
    return pl.multiple_of(block * SHARE, SHARE)


def rows_kernel(*refs):
    pos_ref, wg_ref, wu_ref, wd_ref = refs[:4]
    x_pieces, s_pieces = refs[4:14], refs[14:24]
    own_a, own_b, send_a, send_b, d_ref, h_ref, score_ref = refs[24:31]
    w_all, xs, ss, acc, rs, w_sem, x_sem, s_sem, r_sem = refs[31:]
    w_copies = [
        pltpu.make_async_copy(w, w_all.at[pl.ds(i * HID, HID)], w_sem.at[i])
        for i, w in enumerate((wg_ref, wu_ref, wd_ref))
    ]
    for copy in w_copies:
        copy.start()
    load_rows(pos_ref, x_pieces, False, xs, x_sem)
    load_rows(pos_ref, s_pieces, True, ss, s_sem)
    acc[...] = jnp.zeros_like(acc)
    for copy in w_copies:
        copy.wait()
    last_dims = (((1,), (1,)), ((), ()))

    def forward(j, carry):
        columns = pl.ds(column_of(pos_ref, j), SHARE)
        await_slot(xs, x_sem, j)
        acc[: 2 * HID] += lax.dot_general(
            w_all[: 2 * HID, columns], xs[j], last_dims, preferred_element_type=F32
        )
        await_slot(ss, s_sem, j)
        acc[2 * HID :] += lax.dot_general(
            w_all[2 * HID :, columns], ss[j], last_dims, preferred_element_type=F32
        )
        return carry

    lax.fori_loop(0, 8, forward, 0)
    pre_gate, pre_up, back = acc[:HID], acc[HID : 2 * HID], acc[2 * HID :]
    tanh_part = jnp.tanh(
        SQRT_TWO_PI * (pre_gate + CUBIC * pre_gate * pre_gate * pre_gate)
    )
    gelu = 0.5 * pre_gate * (1.0 + tanh_part)
    slope = 0.5 * (1.0 + tanh_part) + 0.5 * pre_gate * (
        1.0 - tanh_part * tanh_part
    ) * SQRT_TWO_PI * (1.0 + 3.0 * CUBIC * pre_gate * pre_gate)
    hidden = (gelu * pre_up).astype(BF16)
    h_ref[...] = hidden
    score_ref[...] = jnp.sum(hidden.astype(F32) * back, axis=0, keepdims=True)
    d_gate = back * pre_up * slope
    d_up = back * gelu
    d_ref[:HID] = d_gate.astype(BF16)
    d_ref[HID:] = d_up.astype(BF16)
    d_rows = jnp.concatenate([d_gate, d_up], axis=0).T.astype(BF16)
    xl = pos_ref[1]

    def backward(j, carry):
        columns = pl.ds(column_of(pos_ref, j), SHARE)
        rs[j] = jnp.dot(
            d_rows, w_all[: 2 * HID, columns], preferred_element_type=F32
        ).astype(BF16)
        parity, iy = j // 4, j % 4
        for x_half in range(2):
            ix = jnp.where(parity == 0, 3 * x_half, 1 + (x_half + xl) % 2)
            for core in range(2):
                for z in range(2):
                    row = ((x_half * 2 + core) * 2 + z) * BLOCK
                    out = ((own_a, own_b), (send_a, send_b))[core][z]
                    place = out.at[ix, iy] if z == 0 else out.at[iy, ix]
                    pltpu.make_async_copy(
                        rs.at[j, pl.ds(row, BLOCK)], place, r_sem.at[j]
                    ).start()
        return carry

    lax.fori_loop(0, 8, backward, 0)

    def drain(j, carry):
        await_slot(rs, r_sem, j)
        return carry

    lax.fori_loop(0, 8, drain, 0)


def weights_kernel(outputs, by_x_first, *refs):
    pos_ref, d_ref = refs[:2]
    pieces, outs = refs[2:12], refs[12 : 12 + outputs]
    xs, gs, x_sem, g_sem = refs[12 + outputs :]
    load_rows(pos_ref, pieces, by_x_first, xs, x_sem)

    def copies(j):
        columns = pl.ds(column_of(pos_ref, j), SHARE)
        return [
            pltpu.make_async_copy(
                gs.at[j, pl.ds(i * HID, HID)], outs[i].at[:, columns], g_sem.at[j, i]
            )
            for i in range(outputs)
        ]

    def step(j, carry):
        await_slot(xs, x_sem, j)
        gs[j] = jnp.dot(d_ref[...], xs[j], preferred_element_type=F32).astype(BF16)
        for copy in copies(j):
            copy.start()
        return carry

    lax.fori_loop(0, 8, step, 0)

    def drain(j, carry):
        for copy in copies(j):
            copy.wait()
        return carry

    lax.fori_loop(0, 8, drain, 0)


SMEM = pl.BlockSpec(memory_space=pltpu.SMEM)
VMEM = pl.BlockSpec(memory_space=pltpu.VMEM)
ANY = pl.BlockSpec(memory_space=pl.ANY)


def shape(dims, dtype=BF16):
    return jax.ShapeDtypeStruct(dims, dtype)


def params():
    return pltpu.CompilerParams(vmem_limit_bytes=VMEM_LIMIT)


def weights_call(outputs, by_x_first, pos, d, pieces):
    return pl.pallas_call(
        functools.partial(weights_kernel, outputs, by_x_first),
        out_shape=[shape((HID, WIDTH))] * outputs,
        in_specs=[SMEM, VMEM] + [ANY] * 10,
        out_specs=[ANY] * outputs,
        scratch_shapes=[
            pltpu.VMEM((8, ROWS, SHARE), BF16),
            pltpu.VMEM((8, outputs * HID, SHARE), BF16),
            pltpu.SemaphoreType.DMA((8,)),
            pltpu.SemaphoreType.DMA((8, outputs)),
        ],
        compiler_params=params(),
        cost_estimate=pl.CostEstimate(
            flops=2 * outputs * HID * ROWS * WIDTH,
            bytes_accessed=2 * WIDTH * (ROWS + outputs * HID),
            transcendentals=0,
        ),
    )(pos, d, *pieces)


def gather_first(t, axis):
    return jnp.stack([t] + [fetch(t, axis, d, 4) for d in OFFSET[1:]])


def gather_last(t, axis):
    nxt, prev = fetch(t, axis, 1, 4), fetch(t, axis, -1, 4)
    half0, half1 = fetch(prev[:2], axis, -1, 4), fetch(nxt[2:], axis, 1, 4)
    return [t, nxt, prev, half0, half1]


def scatter_sum(parts, axis):
    return add(parts[0], *[fetch(parts[i], axis, -OFFSET[i], 4) for i in range(1, 4)])


def body(tokens, grad_out, expert_ids, slot_ids, gate_weights, gate_proj, up_proj, down_proj):
    pos = jnp.stack(
        [lax.axis_index("e"), lax.axis_index("xl"), lax.axis_index("y")]
    ).astype(jnp.int32)
    packed = pl.pallas_call(
        pack_kernel,
        out_shape=[shape((2, CAP, SHARE))] * EXPERTS,
        in_specs=[SMEM] + [VMEM] * 5,
        out_specs=[VMEM] * EXPERTS,
    )(pos, expert_ids, slot_ids, gate_weights, tokens, grad_out)
    mine = jnp.concatenate(
        [packed[0]] + [fetch(packed[k], "e", -k, 4) for k in range(1, 4)], axis=1
    )
    other = fetch(mine, "zl", 1, 2)
    both = jnp.concatenate([mine, other], axis=1)
    x_pieces = gather_last(gather_first(both[0], "y"), XAXES)
    s_pieces = gather_last(gather_first(both[1], XAXES), "y")
    x_pieces = x_pieces + [fetch(t, "c", 1, 2) for t in x_pieces]
    s_pieces = s_pieces + [fetch(t, "c", 1, 2) for t in s_pieces]

    wg, wu, wd = gate_proj[0], up_proj[0], down_proj[0]
    own_a, own_b, send_a, send_b, d, hidden, score = pl.pallas_call(
        rows_kernel,
        out_shape=[shape((4, 4, BLOCK, SHARE))] * 4
        + [shape((2 * HID, ROWS)), shape((HID, ROWS)), shape((1, ROWS), F32)],
        in_specs=[SMEM] + [ANY] * 23,
        out_specs=[ANY] * 4 + [VMEM] * 3,
        scratch_shapes=[
            pltpu.VMEM((3 * HID, WIDTH), BF16),
            pltpu.VMEM((8, ROWS, SHARE), BF16),
            pltpu.VMEM((8, ROWS, SHARE), BF16),
            pltpu.VMEM((3 * HID, ROWS), F32),
            pltpu.VMEM((8, ROWS, SHARE), BF16),
            pltpu.SemaphoreType.DMA((3,)),
            pltpu.SemaphoreType.DMA((8,)),
            pltpu.SemaphoreType.DMA((8,)),
            pltpu.SemaphoreType.DMA((8,)),
        ],
        compiler_params=params(),
        cost_estimate=pl.CostEstimate(
            flops=2 * 5 * HID * ROWS * WIDTH,
            bytes_accessed=2 * WIDTH * (3 * ROWS + 3 * HID),
            transcendentals=HID * ROWS,
        ),
    )(pos, wg, wu, wd, *x_pieces, *s_pieces)

    recv_a, recv_b = fetch(send_a, "c", 1, 2), fetch(send_b, "c", 1, 2)
    part_a = scatter_sum([add(own_a[i], recv_a[i]) for i in range(4)], XAXES)
    part_b = scatter_sum([add(own_b[i], recv_b[i]) for i in range(4)], "y")
    part_a = scatter_sum([part_a[i] for i in range(4)], "y")
    part_b = scatter_sum([part_b[i] for i in range(4)], XAXES)
    rows = add(part_a, fetch(part_b, "zl", 1, 2))
    back_rows = [rows[:CAP]] + [
        fetch(rows[k * CAP : (k + 1) * CAP], "e", k, 4) for k in range(1, 4)
    ]

    score = score.reshape(2, 2, 2, BLOCK)
    score = score[:, 0] + fetch(score[:, 1], "c", 1, 2)
    score = score[:, 0] + fetch(score[:, 1], "zl", 1, 2)
    score = score[0:1] + fetch(score[1:2], XAXES, 2, 4)
    score = score + fetch(score, "xl", 1, 2)
    score = score + fetch(score, "y", 2, 4)
    score = score + lax.ppermute(score, "y", [(0, 1), (1, 0), (2, 3), (3, 2)])
    back_scores = [score[:, :CAP]] + [
        fetch(score[:, k * CAP : (k + 1) * CAP], "e", k, 4) for k in range(1, 4)
    ]

    (grad_down,) = weights_call(1, True, pos, hidden, s_pieces)
    grad_gate, grad_up = weights_call(2, False, pos, d, x_pieces)

    grad_tokens, grad_gates = pl.pallas_call(
        combine_kernel,
        out_shape=[shape((TOK, SHARE)), shape((TOK, 2), F32)],
        in_specs=[SMEM] + [VMEM] * 11,
        out_specs=[VMEM] * 2,
    )(pos, expert_ids, slot_ids, gate_weights, *back_scores, *back_rows)
    return (grad_tokens, grad_gates, grad_gate[None], grad_up[None], grad_down[None])


def solution(mesh):
    parts = Mesh(
        mesh.devices.reshape(4, 2, 2, 2, 2, 4), ("e", "zl", "xh", "c", "xl", "y")
    )
    ex, mp = ("e", "zl", "xh", "c"), ("xl", "y")
    return jax.shard_map(
        body,
        mesh=parts,
        in_specs=(
            P(ex, mp),
            P(ex, mp),
            P(ex, None),
            P(ex, None),
            P(ex, None),
            P(ex, mp, None),
            P(ex, mp, None),
            P(ex, mp, None),
        ),
        out_specs=(
            P(ex, mp),
            P(ex, None),
            P(ex, mp, None),
            P(ex, mp, None),
            P(ex, mp, None),
        ),
        check_vma=False,
    )
```

```python
import functools

import jax
import jax.numpy as jnp
from jax import lax
from jax.experimental import pallas as pl
from jax.experimental.pallas import tpu as pltpu
from jax.sharding import Mesh
from jax.sharding import PartitionSpec as P

SQRT_TWO_PI = 0.7978845608028654
CUBIC = 0.044715

EXPERTS = 4
CAP = 20
TOK = 32
SHARE = 640
WIDTH = 5120
HID = 160
BLOCK = EXPERTS * CAP
ROWS = 8 * BLOCK
HALF = ROWS // 2
TALL = BLOCK + 8
XAXES = ("xh", "xl")

BF16 = jnp.bfloat16
F32 = jnp.float32

OFFSET = (0, 1, -1, 2)


def fetch(value, axis, offset, size):
    return lax.ppermute(value, axis, [((i + offset) % size, i) for i in range(size)])


def add(*terms):
    total = terms[0].astype(F32)
    for term in terms[1:]:
        total = total + term.astype(F32)
    return total.astype(BF16)


def targets_of(pos_ref, eid_ref, sid_ref):
    relative = (eid_ref[...] - pos_ref[0] + EXPERTS) % EXPERTS
    return jnp.where(sid_ref[...] >= 0, relative * CAP + sid_ref[...], -1)


def pack_kernel(pos_ref, eid_ref, sid_ref, gate_ref, tok_ref, up_ref, *outs):
    target = targets_of(pos_ref, eid_ref, sid_ref)
    gate = gate_ref[...].astype(F32)
    slot = lax.broadcasted_iota(jnp.int32, (CAP, TOK), 0)
    for k in range(EXPERTS):
        first = target[0:1] == slot + k * CAP
        second = target[1:2] == slot + k * CAP
        one = jnp.where(first, 1.0, jnp.where(second, 1.0, 0.0)).astype(BF16)
        scale = jnp.where(
            first, gate[0:1], jnp.where(second, gate[1:2], 0.0)
        ).astype(BF16)
        outs[k][0] = jnp.dot(
            one, tok_ref[...], preferred_element_type=F32
        ).astype(BF16)
        outs[k][1] = jnp.dot(
            scale, up_ref[...], preferred_element_type=F32
        ).astype(BF16)


def combine_kernel(pos_ref, eid_ref, sid_ref, gate_ref, *refs):
    blocks, (tok_ref, gates_ref) = refs[:8], refs[8:]
    target = targets_of(pos_ref, eid_ref, sid_ref)
    slot = lax.broadcasted_iota(jnp.int32, (CAP, TOK), 0)
    every = lax.broadcasted_iota(jnp.int32, (BLOCK, TOK), 0)
    lane = lax.broadcasted_iota(jnp.int32, (1, BLOCK), 1)
    total = jnp.zeros((TOK, SHARE), F32)
    score = jnp.zeros((1, BLOCK), F32)
    for i, block in enumerate(blocks):
        k = i % EXPERTS
        hits = [target[c : c + 1] == slot + k * CAP for c in range(2)]
        one = jnp.where(hits[0], 1.0, jnp.where(hits[1], 1.0, 0.0)).astype(BF16)
        total = total + lax.dot_general(
            one, block[0:CAP], (((0,), (0,)), ((), ())), preferred_element_type=F32
        )
        here = jnp.logical_and(lane >= k * CAP, lane < (k + 1) * CAP)
        score = score + jnp.where(here, block[CAP : CAP + 1, 0:BLOCK].astype(F32), 0.0)
    tok_ref[...] = total.astype(BF16)
    for c in range(2):
        chosen = jnp.where(target[c : c + 1] == every, 1.0, 0.0)
        gates_ref[c : c + 1] = jnp.dot(
            score, chosen, precision=lax.Precision.HIGHEST, preferred_element_type=F32
        ) / gate_ref[c : c + 1].astype(F32)


def stack_kernel(*refs):
    sources, outs, token_ref = refs[:8], refs[8:10], refs[10]
    for i in range(8):
        outs[i // 4][i % 4] = sources[i][...]
    token_ref[...] = jnp.zeros_like(token_ref)


def join_kernel(token_ref, wg_ref, wu_ref, wd_ref, w_ref, sem):
    del token_ref
    copies = [
        pltpu.make_async_copy(w, w_ref.at[pl.ds(i * HID, HID)], sem.at[i])
        for i, w in enumerate((wg_ref, wu_ref, wd_ref))
    ]
    for copy in copies:
        copy.start()
    for copy in copies:
        copy.wait()


def row_of(pos_ref, core, ix):
    xl = pos_ref[1]
    x_half = (0, xl, 1 - xl, 1)[ix]
    row = core * HALF + x_half * 2 * BLOCK
    return row if isinstance(row, int) else pl.multiple_of(row, 2 * BLOCK)


def place_rows(pos_ref, pieces, by_x_first, place, slots):
    for core in range(2):
        for last in range(4):
            for inner in range(4):
                ix, iy = (inner, last) if by_x_first else (last, inner)
                slot = place((1 if ix in (1, 2) else 0) * 4 + iy)
                if slot is None:
                    continue
                if last < 3:
                    piece = pieces[core][last][inner]
                else:
                    piece = pieces[core][3 + inner // 2][inner % 2]
                slots[slot, pl.ds(row_of(pos_ref, core, ix), 2 * BLOCK)] = piece


def columns_of(pos_ref, parity, iy):
    xl, y = pos_ref[1], pos_ref[2]
    offset = jnp.where(iy == 1, 1, jnp.where(iy == 2, 3, jnp.where(iy == 3, 2, 0)))
    block = ((xl + parity) % 2) * 4 + (y + offset) % 4
    return pl.ds(pl.multiple_of(block * SHARE, SHARE), SHARE)


LAST_DIMS = (((1,), (1,)), ((), ()))


def accumulate(pos_ref, acc, w_all, xs, ss, x_slots, s_slots):
    def x_step(t, carry):
        acc[: 2 * HID] += lax.dot_general(
            w_all[: 2 * HID, columns_of(pos_ref, *x_slots[1](t))],
            xs[t],
            LAST_DIMS,
            preferred_element_type=F32,
        )
        return carry

    def s_step(t, carry):
        acc[2 * HID :] += lax.dot_general(
            w_all[2 * HID :, columns_of(pos_ref, *s_slots[1](t))],
            ss[t],
            LAST_DIMS,
            preferred_element_type=F32,
        )
        return carry

    lax.fori_loop(0, x_slots[0], x_step, 0)
    lax.fori_loop(0, s_slots[0], s_step, 0)


def early_kernel(*refs):
    pos_ref, w_all = refs[:2]
    x_pieces, s_pieces = (refs[2:5], refs[5:8]), (refs[8:10], refs[10:12])
    acc, xs, ss = refs[12:]
    place_rows(
        pos_ref,
        x_pieces,
        True,
        lambda j: (j // 4) * 3 + j % 4 if j % 4 < 3 else None,
        xs,
    )
    place_rows(
        pos_ref,
        [(None,) + tuple(s) for s in s_pieces],
        False,
        lambda j: j - 4 if j >= 4 else None,
        ss,
    )
    acc[...] = jnp.zeros_like(acc)
    accumulate(
        pos_ref, acc, w_all, xs, ss,
        (6, lambda t: (t // 3, t % 3)), (4, lambda t: (1, t)),
    )


def late_kernel(*refs):
    pos_ref, w_all, early_ref = refs[:3]
    x_pieces, s_pieces = (refs[3:5], refs[5:7]), (refs[7:10], refs[10:13])
    xs, ss, out_a, out_b, d_ref, h_ref, rows_ref, score_ref, acc = refs[13:]
    place_rows(
        pos_ref,
        [(None,) * 3 + tuple(x) for x in x_pieces],
        True,
        lambda j: j // 4 if j % 4 == 3 else None,
        xs,
    )
    place_rows(
        pos_ref,
        [(s[0], None, None, s[1], s[2]) for s in s_pieces],
        False,
        lambda j: j if j < 4 else None,
        ss,
    )
    acc[...] = early_ref[...]
    accumulate(
        pos_ref, acc, w_all, xs, ss, (2, lambda t: (t, 3)), (4, lambda t: (0, t))
    )
    pre_gate, pre_up, back = acc[:HID], acc[HID : 2 * HID], acc[2 * HID :]
    tanh_part = jnp.tanh(
        SQRT_TWO_PI * (pre_gate + CUBIC * pre_gate * pre_gate * pre_gate)
    )
    gelu = 0.5 * pre_gate * (1.0 + tanh_part)
    slope = 0.5 * (1.0 + tanh_part) + 0.5 * pre_gate * (
        1.0 - tanh_part * tanh_part
    ) * SQRT_TWO_PI * (1.0 + 3.0 * CUBIC * pre_gate * pre_gate)
    hidden = (gelu * pre_up).astype(BF16)
    h_ref[...] = hidden
    score = jnp.sum(hidden.astype(F32) * back, axis=0, keepdims=True)
    score = jnp.broadcast_to(score, (8, ROWS))
    for b in range(8):
        turned = score if b == 0 else pltpu.roll(score, ROWS - b * BLOCK, 1)
        score_ref[b] = turned.astype(BF16)
    d_gate = back * pre_up * slope
    d_up = back * gelu
    d_ref[:HID] = d_gate.astype(BF16)
    d_ref[HID:] = d_up.astype(BF16)
    rows_ref[...] = jnp.concatenate([d_gate, d_up], axis=0).T.astype(BF16)
    row_sums(1, pos_ref, w_all, rows_ref, score_ref, out_a, out_b)


def row_sums(core, pos_ref, w_all, rows_ref, score_ref, out_a, out_b):
    xl = pos_ref[1]

    def step(j, carry):
        parity, iy = j // 4, j % 4
        value = jnp.dot(
            rows_ref[core * HALF : (core + 1) * HALF],
            w_all[: 2 * HID, columns_of(pos_ref, parity, iy)],
            preferred_element_type=F32,
        ).astype(BF16)
        for x_half in range(2):
            ix = jnp.where(parity == 0, 3 * x_half, 1 + (x_half + xl) % 2)
            for z in range(2):
                b = x_half * 2 + z
                out, place = (out_a, (ix, iy)) if z == 0 else (out_b, (iy, ix))
                out[(*place, slice(0, BLOCK))] = value[b * BLOCK : (b + 1) * BLOCK]
                out[(*place, slice(BLOCK, TALL))] = score_ref[core * 4 + b]
        return carry

    lax.fori_loop(0, 8, step, 0)


def rows_kernel(pos_ref, w_all, rows_ref, score_ref, out_a, out_b):
    row_sums(0, pos_ref, w_all, rows_ref, score_ref, out_a, out_b)


def weights_kernel(outputs, slots, *refs):
    pos_ref, d_ref, arrays = refs[0], refs[1], refs[2:4]
    outs, token_ref = refs[4 : 4 + outputs], refs[4 + outputs]
    gs, g_sem = refs[5 + outputs :]
    token_ref[...] = jnp.zeros_like(token_ref)
    done = 0
    for array, (count, features) in zip(arrays, slots):

        def copies(t):
            columns = columns_of(pos_ref, *features(t))
            return [
                pltpu.make_async_copy(
                    gs.at[done + t, pl.ds(i * HID, HID)],
                    outs[i].at[:, columns],
                    g_sem.at[done + t, i],
                )
                for i in range(outputs)
            ]

        def step(t, carry):
            gs[done + t] = jnp.dot(
                d_ref[...], array[t], preferred_element_type=F32
            ).astype(BF16)
            for copy in copies(t):
                copy.start()
            return carry

        lax.fori_loop(0, count, step, 0)
        done += count

    def drain(t, carry):
        for i in range(outputs):
            part = gs.at[t, pl.ds(i * HID, HID)]
            pltpu.make_async_copy(part, part, g_sem.at[t, i]).wait()
        return carry

    lax.fori_loop(0, 8, drain, 0)


def sum_kernel(*refs):
    parts, outs = refs[2:10], refs[10:]
    for side in range(2):
        for i in range(4):
            total = parts[4 * side][i].astype(F32)
            for part in parts[4 * side + 1 : 4 * side + 4]:
                total = total + part[i].astype(F32)
            outs[4 * side + i][...] = total.astype(BF16)


def nothing_kernel(*refs):
    pass


SMEM = pl.BlockSpec(memory_space=pltpu.SMEM)
VMEM = pl.BlockSpec(memory_space=pltpu.VMEM)
ANY = pl.BlockSpec(memory_space=pl.ANY)
DMA = pltpu.SemaphoreType.DMA


def shape(dims, dtype=BF16):
    return jax.ShapeDtypeStruct(dims, dtype)


def params(mib):
    return pltpu.CompilerParams(vmem_limit_bytes=mib * 1024 * 1024)


def cost(products, size):
    return pl.CostEstimate(flops=2 * products, bytes_accessed=size, transcendentals=0)


TOKEN = shape((8, 128), F32)


def tie(*values):
    return pl.pallas_call(
        nothing_kernel,
        out_shape=[shape(v.shape, v.dtype) for v in values],
        in_specs=[VMEM] * len(values),
        out_specs=[VMEM] * len(values),
        input_output_aliases={i: i for i in range(len(values))},
        compiler_params=params(4),
    )(*values)


def weights_call(outputs, slots, pos, d, arrays):
    return pl.pallas_call(
        functools.partial(weights_kernel, outputs, slots),
        out_shape=[shape((HID, WIDTH))] * outputs + [TOKEN],
        in_specs=[SMEM] + [VMEM] * 3,
        out_specs=[ANY] * outputs + [VMEM],
        scratch_shapes=[
            pltpu.VMEM((8, outputs * HID, SHARE), BF16),
            DMA((8, outputs)),
        ],
        compiler_params=params(10),
        cost_estimate=cost(
            outputs * HID * ROWS * WIDTH, 2 * WIDTH * (ROWS + outputs * HID)
        ),
    )(pos, d, *arrays)


def scatter_sum(parts, axis):
    return [parts[0]] + [fetch(parts[i], axis, -OFFSET[i], 4) for i in range(1, 4)]


def between(value, k, dz):
    pairs = [
        ((((e + k) % 4) * 2 + (z ^ dz)), e * 2 + z) for e in range(4) for z in range(2)
    ]
    return lax.ppermute(value, ("e", "zl"), pairs)


def body(tokens, grad_out, expert_ids, slot_ids, gate_weights, gate_proj, up_proj, down_proj):
    pos = jnp.stack(
        [lax.axis_index("e"), lax.axis_index("xl"), lax.axis_index("y")]
    ).astype(jnp.int32)
    routes = (expert_ids.T, slot_ids.T, gate_weights.T)
    packed = pl.pallas_call(
        pack_kernel,
        out_shape=[shape((2, CAP, SHARE))] * EXPERTS,
        in_specs=[SMEM] + [VMEM] * 5,
        out_specs=[VMEM] * EXPERTS,
        compiler_params=params(4),
    )(pos, *routes, tokens, grad_out)
    arrived = [packed[0]] + [
        between(packed[k], -k, dz)
        for dz in range(2)
        for k in range(EXPERTS)
        if dz + k > 0
    ]
    both = jnp.concatenate(arrived, axis=1)
    x, s = both[0], both[1]
    x_first = [x] + [fetch(x, XAXES, d, 4) for d in OFFSET[1:]]
    s_first = [s] + [fetch(s, "y", d, 4) for d in OFFSET[1:]]
    x, s, token = pl.pallas_call(
        stack_kernel,
        out_shape=[shape((4, 2 * BLOCK, SHARE))] * 2 + [TOKEN],
        in_specs=[VMEM] * 8,
        out_specs=[VMEM] * 3,
        compiler_params=params(6),
    )(*x_first, *s_first)
    w_all = pl.pallas_call(
        join_kernel,
        out_shape=shape((3 * HID, WIDTH)),
        in_specs=[VMEM] + [ANY] * 3,
        out_specs=VMEM,
        scratch_shapes=[DMA((3,))],
        compiler_params=params(4),
        cost_estimate=cost(0, 12 * HID * WIDTH),
    )(token, gate_proj[0], up_proj[0], down_proj[0])
    x_own = [x, fetch(x, "y", 1, 4), fetch(x, "y", -1, 4)]
    s_own = [s, fetch(s, XAXES, 1, 4), fetch(s, XAXES, -1, 4)]
    x_pair = [fetch(t, "c", 1, 2) for t in x_own]
    s_pair = [fetch(t, "c", 1, 2) for t in s_own]
    x_own += [fetch(x_own[2][:2], "y", -1, 4), fetch(x_own[1][2:], "y", 1, 4)]
    s_own += [fetch(s_own[2][:2], XAXES, -1, 4), fetch(s_own[1][2:], XAXES, 1, 4)]
    early, xs_early, ss_early = pl.pallas_call(
        early_kernel,
        out_shape=[
            shape((3 * HID, ROWS), F32),
            shape((6, ROWS, SHARE)),
            shape((4, ROWS, SHARE)),
        ],
        in_specs=[SMEM] + [VMEM] * 11,
        out_specs=[VMEM] * 3,
        compiler_params=params(10),
        cost_estimate=cost(
            2 * HID * ROWS * WIDTH, 2 * WIDTH * (3 * HID + ROWS * 5 // 4)
        ),
    )(pos, w_all, *x_own[:3], *x_pair[:3], *s_own[1:3], *s_pair[1:3])
    early, x_own[3], x_own[4], s_own[3], s_own[4] = tie(
        early, *x_own[3:], *s_own[3:]
    )
    x_pair += [fetch(t, "c", 1, 2) for t in x_own[3:]]
    s_pair += [fetch(t, "c", 1, 2) for t in s_own[3:]]
    sums = [shape((4, 4, TALL, SHARE))] * 2
    xs_late, ss_late, send_a, send_b, d, hidden, rows, score = pl.pallas_call(
        late_kernel,
        out_shape=[shape((2, ROWS, SHARE)), shape((4, ROWS, SHARE))]
        + sums
        + [
            shape((2 * HID, ROWS)),
            shape((HID, ROWS)),
            shape((ROWS, 2 * HID)),
            shape((8, 8, ROWS)),
        ],
        in_specs=[SMEM] + [VMEM] * 12,
        out_specs=[VMEM] * 8,
        scratch_shapes=[pltpu.VMEM((3 * HID, ROWS), F32)],
        compiler_params=params(16),
        cost_estimate=cost(
            2 * HID * ROWS * WIDTH, 2 * WIDTH * (3 * HID + ROWS * 5 // 4)
        ),
    )(
        pos, w_all, early,
        *x_own[3:], *x_pair[3:], s_own[0], *s_own[3:], s_pair[0], *s_pair[3:],
    )
    recv_a, recv_b = fetch(send_a, "c", 1, 2), fetch(send_b, "c", 1, 2)
    own_a, own_b = pl.pallas_call(
        rows_kernel,
        out_shape=sums,
        in_specs=[SMEM] + [VMEM] * 3,
        out_specs=[VMEM] * 2,
        compiler_params=params(8),
        cost_estimate=cost(
            2 * HID * HALF * WIDTH, 2 * WIDTH * (HALF + 2 * HID)
        ),
    )(pos, w_all, rows, score)
    part_a = [add(own_a[i], recv_a[i]) for i in range(4)]
    part_b = [add(own_b[i], recv_b[i]) for i in range(4)]
    hidden, d, part_a[0], part_b[0] = tie(hidden, d, part_a[0], part_b[0])
    grad_down, token_s = weights_call(
        1, ((4, lambda t: (1, t)), (4, lambda t: (0, t))), pos, hidden, (ss_early, ss_late)
    )
    grad_gate, grad_up, token_x = weights_call(
        2, ((6, lambda t: (t // 3, t % 3)), (2, lambda t: (t, 3))), pos, d, (xs_early, xs_late)
    )
    parts = pl.pallas_call(
        sum_kernel,
        out_shape=[shape((TALL, SHARE))] * 8,
        in_specs=[VMEM] * 10,
        out_specs=[VMEM] * 8,
        compiler_params=params(6),
    )(token_s, token_x, *scatter_sum(part_a, XAXES), *scatter_sum(part_b, "y"))
    part_a = add(*scatter_sum(parts[:4], "y"))
    part_b = add(*scatter_sum(parts[4:], XAXES))
    blocks = []
    for dz, part in enumerate((part_a, part_b)):
        for k in range(EXPERTS):
            block = jnp.concatenate(
                [part[k * CAP : (k + 1) * CAP], part[BLOCK : BLOCK + 1]]
            )
            blocks.append(between(block, k, dz) if dz + k > 0 else block)

    grad_tokens, grad_gates = pl.pallas_call(
        combine_kernel,
        out_shape=[shape((TOK, SHARE)), shape((2, TOK), F32)],
        in_specs=[SMEM] + [VMEM] * 11,
        out_specs=[VMEM] * 2,
        compiler_params=params(4),
    )(pos, *routes, *blocks)
    return (grad_tokens, grad_gates.T, grad_gate[None], grad_up[None], grad_down[None])


def solution(mesh):
    parts = Mesh(
        mesh.devices.reshape(4, 2, 2, 2, 2, 4), ("e", "zl", "xh", "c", "xl", "y")
    )
    ex, mp = ("e", "zl", "xh", "c"), ("xl", "y")
    return jax.shard_map(
        body,
        mesh=parts,
        in_specs=(
            P(ex, mp),
            P(ex, mp),
            P(ex, None),
            P(ex, None),
            P(ex, None),
            P(ex, mp, None),
            P(ex, mp, None),
            P(ex, mp, None),
        ),
        out_specs=(
            P(ex, mp),
            P(ex, None),
            P(ex, mp, None),
            P(ex, mp, None),
            P(ex, mp, None),
        ),
        check_vma=False,
    )
```

```python
import functools

import jax
import jax.numpy as jnp
from jax import lax
from jax.experimental import pallas as pl
from jax.experimental.pallas import tpu as pltpu
from jax.sharding import Mesh
from jax.sharding import PartitionSpec as P

SQRT_TWO_PI = 0.7978845608028654
CUBIC = 0.044715

EXPERTS = 4
CAP = 20
TOK = 32
SHARE = 640
WIDTH = 5120
HID = 160
BLOCK = EXPERTS * CAP
ROWS = 8 * BLOCK
CHIP = 4 * BLOCK
PART = 2 * BLOCK
TALL = PART + 8
XAXES = ("xh", "xl")

BF16 = jnp.bfloat16
F32 = jnp.float32

OFFSET = (0, 1, -1, 2)


def fetch(value, axis, offset, size):
    return lax.ppermute(value, axis, [((i + offset) % size, i) for i in range(size)])


def cross(value, first, offset):
    pairs = []
    for i in range(32):
        xh, core, xl, y = i // 16, i // 8 % 2, i // 4 % 2, i % 4
        x = 2 * xh + xl
        if (core == 0) == first:
            source_x, source_y = (x + offset) % 4, y
        else:
            source_x, source_y = x, (y + offset) % 4
        source = source_x // 2 * 16 + core * 8 + source_x % 2 * 4 + source_y
        pairs.append((source, i))
    return lax.ppermute(value, ("xh", "c", "xl", "y"), pairs)


def add(*terms):
    total = terms[0].astype(F32)
    for term in terms[1:]:
        total = total + term.astype(F32)
    return total.astype(BF16)


def pack_kernel(pos_ref, own_ref, other_ref, own_rows, other_rows, *outs):
    core = pos_ref[2]
    slot = lax.broadcasted_iota(jnp.int32, (CAP, TOK), 0).astype(F32)
    for place, info, rows in ((core, own_ref, own_rows), (1 - core, other_ref, other_rows)):
        target, gate = info[0:2], jnp.where(core == 0, 1.0, info[2:4])
        for k in range(EXPERTS):
            first = target[0:1] == slot + k * CAP
            second = target[1:2] == slot + k * CAP
            scale = jnp.where(
                first, gate[0:1], jnp.where(second, gate[1:2], 0.0)
            ).astype(BF16)
            outs[k][place] = jnp.dot(
                scale, rows[...], preferred_element_type=F32
            ).astype(BF16)


def combine_kernel(info_ref, *refs):
    blocks, (tok_ref, gates_ref) = refs[:EXPERTS], refs[EXPERTS:]
    target = info_ref[0:2]
    slot = lax.broadcasted_iota(jnp.int32, (CAP, TOK), 0).astype(F32)
    every = lax.broadcasted_iota(jnp.int32, (BLOCK, TOK), 0).astype(F32)
    lane = lax.broadcasted_iota(jnp.int32, (1, BLOCK), 1)
    total = jnp.zeros((TOK, SHARE), F32)
    score = jnp.zeros((1, BLOCK), F32)
    for k, block in enumerate(blocks):
        hits = [target[c : c + 1] == slot + k * CAP for c in range(2)]
        one = jnp.where(hits[0], 1.0, jnp.where(hits[1], 1.0, 0.0)).astype(BF16)
        total = total + lax.dot_general(
            one, block[0:CAP], (((0,), (0,)), ((), ())), preferred_element_type=F32
        )
        here = jnp.logical_and(lane >= k * CAP, lane < (k + 1) * CAP)
        score = score + jnp.where(here, block[CAP : CAP + 1, 0:BLOCK].astype(F32), 0.0)
    tok_ref[...] = total.astype(BF16)
    for c in range(2):
        chosen = jnp.where(target[c : c + 1] == every, 1.0, 0.0)
        gates_ref[c : c + 1] = jnp.dot(
            score, chosen, precision=lax.Precision.HIGHEST, preferred_element_type=F32
        ) / info_ref[2 + c : 3 + c]


def stack_kernel(*refs):
    sources, out, token_ref = refs[:4], refs[4], refs[5]
    for i in range(4):
        out[i, 0:BLOCK], out[i, BLOCK:PART] = sources[i][0], sources[i][1]
    token_ref[...] = jnp.zeros_like(token_ref)


def join_kernel(token_ref, wg_ref, wu_ref, wd_ref, w_ref, sem):
    del token_ref
    copies = [
        pltpu.make_async_copy(w, w_ref.at[pl.ds(i * HID, HID)], sem.at[i])
        for i, w in enumerate((wg_ref, wu_ref, wd_ref))
    ]
    for copy in copies:
        copy.start()
    for copy in copies:
        copy.wait()


def place_rows(pos_ref, pieces, by_x_first, place, slots):
    xl = pos_ref[0]
    for last in range(4):
        for inner in range(4):
            ix, iy = (inner, last) if by_x_first else (last, inner)
            slot = place((1 if ix in (1, 2) else 0) * 4 + iy)
            if slot is None:
                continue
            row = (0, xl, 1 - xl, 1)[ix] * CHIP
            if not isinstance(row, int):
                row = pl.multiple_of(row, CHIP)
            slots[slot, pl.ds(row, PART)] = pieces[last][0][inner]
            slots[slot, pl.ds(row + PART, PART)] = pieces[last][1][inner]


def place_both(pos_ref, own, other, x_place, xs, s_place, ss):
    @pl.when(pos_ref[2] == 0)
    def _():
        place_rows(pos_ref, own, True, x_place, xs)
        place_rows(pos_ref, other, False, s_place, ss)

    @pl.when(pos_ref[2] == 1)
    def _():
        place_rows(pos_ref, other, True, x_place, xs)
        place_rows(pos_ref, own, False, s_place, ss)


def columns_of(pos_ref, parity, iy):
    xl, y = pos_ref[0], pos_ref[1]
    offset = jnp.where(iy == 1, 1, jnp.where(iy == 2, 3, jnp.where(iy == 3, 2, 0)))
    block = ((xl + parity) % 2) * 4 + (y + offset) % 4
    return pl.ds(pl.multiple_of(block * SHARE, SHARE), SHARE)


LAST_DIMS = (((1,), (1,)), ((), ()))


def accumulate(pos_ref, acc, w_all, xs, ss, x_slots, s_slots):
    def x_step(t, carry):
        acc[: 2 * HID] += lax.dot_general(
            w_all[: 2 * HID, columns_of(pos_ref, *x_slots[1](t))],
            xs[t],
            LAST_DIMS,
            preferred_element_type=F32,
        )
        return carry

    def s_step(t, carry):
        acc[2 * HID :] += lax.dot_general(
            w_all[2 * HID :, columns_of(pos_ref, *s_slots[1](t))],
            ss[t],
            LAST_DIMS,
            preferred_element_type=F32,
        )
        return carry

    lax.fori_loop(0, x_slots[0], x_step, 0)
    lax.fori_loop(0, s_slots[0], s_step, 0)


def early_kernel(pos_ref, w_all, *refs):
    own, other = [tuple(zip(refs[i : i + 3], refs[i + 3 : i + 6])) for i in (0, 6)]
    acc, xs, ss, token_ref = refs[12:]
    token_ref[...] = jnp.zeros_like(token_ref)
    place_both(
        pos_ref, own, other,
        lambda j: (j // 4) * 3 + j % 4 if j % 4 < 3 else None, xs,
        lambda j: j - 4 if j >= 4 else None, ss,
    )
    acc[...] = jnp.zeros_like(acc)
    accumulate(
        pos_ref, acc, w_all, xs, ss,
        (6, lambda t: (t // 3, t % 3)), (4, lambda t: (1, t)),
    )


def late_kernel(pos_ref, w_all, early_ref, *refs):
    own, other = [
        (refs[i : i + 2], None, None, (refs[i + 2].at[0], refs[i + 2].at[1])) for i in (0, 3)
    ]
    xs, ss, out, d_ref, h_ref, rows_ref, score_ref, acc, lhs = refs[6:]
    place_both(
        pos_ref, own, other,
        lambda j: j // 4 if j % 4 == 3 else None, xs,
        lambda j: j if j < 4 else None, ss,
    )
    acc[...] = early_ref[...]
    accumulate(
        pos_ref, acc, w_all, xs, ss, (2, lambda t: (t, 3)), (4, lambda t: (0, t))
    )
    pre_gate, pre_up, back = acc[:HID], acc[HID : 2 * HID], acc[2 * HID :]
    tanh_part = jnp.tanh(
        SQRT_TWO_PI * (pre_gate + CUBIC * pre_gate * pre_gate * pre_gate)
    )
    gelu = 0.5 * pre_gate * (1.0 + tanh_part)
    slope = 0.5 * (1.0 + tanh_part) + 0.5 * pre_gate * (
        1.0 - tanh_part * tanh_part
    ) * SQRT_TWO_PI * (1.0 + 3.0 * CUBIC * pre_gate * pre_gate)
    hidden = (gelu * pre_up).astype(BF16)
    h_ref[...] = hidden
    score = jnp.sum(hidden.astype(F32) * back, axis=0, keepdims=True)
    score = jnp.broadcast_to(score, (8, ROWS))
    for b, start in enumerate((0, PART, CHIP, CHIP + PART)):
        turned = score if b == 0 else pltpu.roll(score, ROWS - start, 1)
        score_ref[b] = turned.astype(BF16)
    d_gate = back * pre_up * slope
    d_up = back * gelu
    d_ref[:HID] = d_gate.astype(BF16)
    d_ref[HID:] = d_up.astype(BF16)
    rows_ref[...] = jnp.concatenate([d_gate, d_up], axis=0).T.astype(BF16)
    row_sums(1 - pos_ref[2], pos_ref, w_all, rows_ref, score_ref, out, lhs)


def row_sums(z, pos_ref, w_all, rows_ref, score_ref, out, lhs):
    xl = pos_ref[0]
    for x_half in range(2):
        lhs[x_half * PART : (x_half + 1) * PART] = rows_ref[
            pl.ds(pl.multiple_of((2 * x_half + z) * PART, PART), PART)
        ]

    def step(j, carry):
        parity, iy = j // 4, j % 4
        value = jnp.dot(
            lhs[...],
            w_all[: 2 * HID, columns_of(pos_ref, parity, iy)],
            preferred_element_type=F32,
        ).astype(BF16)
        for x_half in range(2):
            ix = jnp.where(parity == 0, 3 * x_half, 1 + (x_half + xl) % 2)
            first, second = jnp.where(z == 0, ix, iy), jnp.where(z == 0, iy, ix)
            out[first, second, 0:PART] = value[x_half * PART : (x_half + 1) * PART]
            out[first, second, PART:TALL] = score_ref[2 * x_half + z]
        return carry

    lax.fori_loop(0, 8, step, 0)


def rows_kernel(pos_ref, w_all, rows_ref, score_ref, out, lhs):
    row_sums(pos_ref[2], pos_ref, w_all, rows_ref, score_ref, out, lhs)


def weights_kernel(outputs, slots, skip, *refs):
    pos_ref, d_ref, arrays = refs[0], refs[1], refs[2:4]
    refs = refs[4 + skip :]
    outs, token_ref, gs, g_sem = refs[:outputs], *refs[outputs:]
    token_ref[...] = jnp.zeros_like(token_ref)
    done = 0
    for array, (count, features) in zip(arrays, slots):

        def copies(t):
            columns = columns_of(pos_ref, *features(t))
            return [
                pltpu.make_async_copy(
                    gs.at[done + t, pl.ds(i * HID, HID)],
                    outs[i].at[:, columns],
                    g_sem.at[done + t, i],
                )
                for i in range(outputs)
            ]

        def step(t, carry):
            gs[done + t] = jnp.dot(
                d_ref[...], array[t], preferred_element_type=F32
            ).astype(BF16)
            for copy in copies(t):
                copy.start()
            return carry

        lax.fori_loop(0, count, step, 0)
        done += count

    def drain(t, carry):
        for i in range(outputs):
            part = gs.at[t, pl.ds(i * HID, HID)]
            pltpu.make_async_copy(part, part, g_sem.at[t, i]).wait()
        return carry

    lax.fori_loop(0, 8, drain, 0)


def relay_kernel(token, part1, arrival1, part2, arrival2, out1, out2, token_ref):
    del token
    token_ref[...] = jnp.zeros_like(token_ref)
    for t in range(2):
        out1[t] = (part1[t].astype(F32) + arrival1[t].astype(F32)).astype(BF16)
        out2[t] = (part2[t].astype(F32) + arrival2[t].astype(F32)).astype(BF16)


def sum_kernel(token, own, next0, next1, prev0, prev1, *outs):
    del token
    for i, out in enumerate(outs):
        total = own[i].astype(F32)
        total = total + (next0, next1)[i // 2][i % 2].astype(F32)
        total = total + (prev0, prev1)[i // 2][i % 2].astype(F32)
        out[...] = total.astype(BF16)


def homes_kernel(pos_ref, *refs):
    parts, outs, total = refs[:4], refs[4:6], refs[6]
    total[...] = (
        parts[0][...].astype(F32)
        + parts[1][...].astype(F32)
        + parts[2][...].astype(F32)
        + parts[3][...].astype(F32)
    )
    scores = total[PART:TALL]
    turned = pltpu.roll(scores, SHARE - BLOCK, 1)
    for out, core in zip(outs, (1 - pos_ref[2], pos_ref[2])):
        row = pl.multiple_of(core * BLOCK, BLOCK)
        out[0:BLOCK] = total[pl.ds(row, BLOCK)].astype(BF16)
        out[BLOCK : BLOCK + 8] = jnp.where(core == 0, scores, turned).astype(BF16)


def split_kernel(a_ref, b_ref, *outs):
    total = a_ref[...].astype(F32) + b_ref[...].astype(F32)
    for k, out in enumerate(outs):
        out[0:CAP] = total[k * CAP : (k + 1) * CAP].astype(BF16)
        out[CAP : CAP + 8] = total[BLOCK : BLOCK + 8].astype(BF16)


def pass_kernel(*refs):
    for z in range(2):
        for t in range(4):
            refs[5][z, t] = refs[1 + 2 * z + t // 2][t % 2]


SMEM = pl.BlockSpec(memory_space=pltpu.SMEM)
VMEM = pl.BlockSpec(memory_space=pltpu.VMEM)
ANY = pl.BlockSpec(memory_space=pl.ANY)
HBM = pl.BlockSpec(memory_space=pltpu.HBM)
DMA = pltpu.SemaphoreType.DMA


def shape(dims, dtype=BF16):
    return jax.ShapeDtypeStruct(dims, dtype)


def params(mib):
    return pltpu.CompilerParams(vmem_limit_bytes=mib * 1024 * 1024)


def cost(products, size):
    return pl.CostEstimate(flops=2 * products, bytes_accessed=size, transcendentals=0)


TOKEN = shape((8, 128), F32)


def weights_call(outputs, slots, pos, d, arrays, after):
    return pl.pallas_call(
        functools.partial(weights_kernel, outputs, slots, len(after)),
        out_shape=[shape((HID, WIDTH))] * outputs + [TOKEN],
        in_specs=[SMEM] + [VMEM] * 3 + [ANY] * len(after),
        out_specs=[ANY] * outputs + [VMEM],
        scratch_shapes=[
            pltpu.VMEM((8, outputs * HID, SHARE), BF16),
            DMA((8, outputs)),
        ],
        compiler_params=params(6),
        cost_estimate=cost(
            outputs * HID * ROWS * WIDTH, 2 * WIDTH * (ROWS + outputs * HID)
        ),
    )(pos, d, *arrays, *after)


def scatter(parts, first):
    return [parts[0]] + [cross(parts[i], first, -OFFSET[i]) for i in range(1, 4)]


def between(value, k, dz):
    pairs = [
        ((((e + k) % 4) * 2 + (z ^ dz)), e * 2 + z) for e in range(4) for z in range(2)
    ]
    return lax.ppermute(value, ("e", "zl"), pairs)


def body(tokens, grad_out, expert_ids, slot_ids, gate_weights, gate_proj, up_proj, down_proj):
    core = lax.axis_index("c")
    pos = jnp.stack([lax.axis_index("xl"), lax.axis_index("y"), core]).astype(jnp.int32)
    relative = (expert_ids.T - lax.axis_index("e") + EXPERTS) % EXPERTS
    target = jnp.where(slot_ids.T >= 0, relative * CAP + slot_ids.T, -1)
    info = jnp.concatenate([target.astype(F32), gate_weights.T.astype(F32)], axis=0)
    keep = jnp.where(core == 0, tokens, grad_out)
    give = jnp.where(core == 0, grad_out, tokens)
    packed = pl.pallas_call(
        pack_kernel,
        out_shape=[shape((2, CAP, SHARE))] * EXPERTS,
        in_specs=[SMEM] + [VMEM] * 4,
        out_specs=[VMEM] * EXPERTS,
        compiler_params=params(2),
    )(pos, info, fetch(info, "c", 1, 2), keep, fetch(give, "c", 1, 2))
    arrived = [packed[0]] + [between(packed[k], -k, 0) for k in range(1, EXPERTS)]
    mine = jnp.concatenate(arrived, axis=1)
    rows = []
    for group in (mine, fetch(mine, "zl", 1, 2)):
        stacked, token = pl.pallas_call(
            stack_kernel,
            out_shape=[shape((4, PART, SHARE)), TOKEN],
            in_specs=[VMEM] * 4,
            out_specs=[VMEM] * 2,
            compiler_params=params(4),
        )(group, *[cross(group, True, d) for d in OFFSET[1:]])
        rows.append(stacked)
    w_all = pl.pallas_call(
        join_kernel,
        out_shape=shape((3 * HID, WIDTH)),
        in_specs=[VMEM] + [HBM] * 3,
        out_specs=VMEM,
        scratch_shapes=[DMA((3,))],
        compiler_params=params(2),
        cost_estimate=cost(0, 12 * HID * WIDTH),
    )(token, gate_proj[0], up_proj[0], down_proj[0])
    own, halves = [], []
    for t in rows:
        nxt, prev = cross(t, False, 1), cross(t, False, -1)
        own += [t, nxt, prev]
        halves += [cross(prev[:2], False, -1), cross(nxt[2:], False, 1)]
    other = [fetch(t, "c", 1, 2) for t in own]
    early, xs_early, ss_early, token = pl.pallas_call(
        early_kernel,
        out_shape=[
            shape((3 * HID, ROWS), F32),
            shape((6, ROWS, SHARE)),
            shape((4, ROWS, SHARE)),
            TOKEN,
        ],
        in_specs=[SMEM] + [VMEM] * 13,
        out_specs=[VMEM] * 4,
        compiler_params=params(4),
        cost_estimate=cost(0, 0),
    )(pos, w_all, *own, *other)
    last = pl.pallas_call(
        pass_kernel,
        out_shape=shape((2, 4, PART, SHARE)),
        in_specs=[ANY] + [VMEM] * 4,
        out_specs=VMEM,
        compiler_params=params(4),
    )(token, *halves)
    sums = shape((4, 4, TALL, SHARE))
    lhs = pltpu.VMEM((ROWS // 2, 2 * HID), BF16)
    xs_late, ss_late, send, d, hidden, d_rows, score = pl.pallas_call(
        late_kernel,
        out_shape=[
            shape((2, ROWS, SHARE)),
            shape((4, ROWS, SHARE)),
            sums,
            shape((2 * HID, ROWS)),
            shape((HID, ROWS)),
            shape((ROWS, 2 * HID)),
            shape((4, 8, ROWS)),
        ],
        in_specs=[SMEM] + [VMEM] * 8,
        out_specs=[VMEM] * 7,
        scratch_shapes=[pltpu.VMEM((3 * HID, ROWS), F32), lhs],
        compiler_params=params(10),
        cost_estimate=cost(
            2 * HID * ROWS * WIDTH, 2 * WIDTH * (3 * HID + ROWS * 5 // 4)
        ),
    )(pos, w_all, early, *rows, last, other[0], other[3], fetch(last, "c", 1, 2))
    recv = fetch(send, "c", 1, 2)
    kept = pl.pallas_call(
        rows_kernel,
        out_shape=sums,
        in_specs=[SMEM] + [VMEM] * 3,
        out_specs=VMEM,
        scratch_shapes=[lhs],
        compiler_params=params(4),
        cost_estimate=cost(
            HID * ROWS * WIDTH, 2 * WIDTH * (ROWS // 2 + 2 * HID)
        ),
    )(pos, w_all, d_rows, score)
    part = add(kept[0], recv[0])
    halves = [
        [add(kept[i, t : t + 2], recv[i, t : t + 2]) for t in (0, 2)] for i in range(1, 4)
    ]
    arrivals = [cross(halves[2][0], True, -1), cross(halves[2][1], True, 1)]
    from_prev, from_next = cross(halves[0][1], True, -1), cross(halves[1][0], True, 1)
    grad_down, token = weights_call(
        1, ((4, lambda t: (1, t)), (4, lambda t: (0, t))), pos, hidden, (ss_early, ss_late),
        (halves[2][0],),
    )
    to_next, to_prev, token = pl.pallas_call(
        relay_kernel,
        out_shape=[shape((2, TALL, SHARE))] * 2 + [TOKEN],
        in_specs=[ANY] + [VMEM] * 4,
        out_specs=[VMEM] * 3,
        compiler_params=params(4),
    )(token, halves[0][0], arrivals[0], halves[1][1], arrivals[1])
    grad_gate, grad_up, token = weights_call(
        2, ((6, lambda t: (t // 3, t % 3)), (2, lambda t: (t, 3))), pos, d, (xs_early, xs_late),
        (token,),
    )
    parts = pl.pallas_call(
        sum_kernel,
        out_shape=[shape((TALL, SHARE))] * 4,
        in_specs=[ANY] + [VMEM] * 5,
        out_specs=[VMEM] * 4,
        compiler_params=params(4),
    )(
        token, part, cross(to_next, True, -1), from_prev, from_next, cross(to_prev, True, 1)
    )
    away, home = pl.pallas_call(
        homes_kernel,
        out_shape=[shape((BLOCK + 8, SHARE))] * 2,
        in_specs=[SMEM] + [VMEM] * 4,
        out_specs=[VMEM] * 2,
        scratch_shapes=[pltpu.VMEM((TALL, SHARE), F32)],
        compiler_params=params(4),
    )(pos, *scatter(parts, False))
    away = lax.ppermute(away, ("zl", "c"), [(0, 1), (2, 3), (1, 2), (3, 0)])
    home = lax.ppermute(home, ("zl", "c"), [(0, 0), (2, 2), (1, 3), (3, 1)])
    blocks = pl.pallas_call(
        split_kernel,
        out_shape=[shape((CAP + 8, SHARE))] * EXPERTS,
        in_specs=[VMEM] * 2,
        out_specs=[VMEM] * EXPERTS,
        compiler_params=params(4),
    )(away, home)
    blocks = [blocks[0]] + [between(blocks[k], k, 0) for k in range(1, EXPERTS)]

    grad_tokens, grad_gates = pl.pallas_call(
        combine_kernel,
        out_shape=[shape((TOK, SHARE)), shape((2, TOK), F32)],
        in_specs=[VMEM] * 5,
        out_specs=[VMEM] * 2,
        compiler_params=params(4),
    )(info, *blocks)
    return (grad_tokens, grad_gates.T, grad_gate[None], grad_up[None], grad_down[None])


def solution(mesh):
    parts = Mesh(
        mesh.devices.reshape(4, 2, 2, 2, 2, 4), ("e", "zl", "xh", "c", "xl", "y")
    )
    ex, mp = ("e", "zl", "xh", "c"), ("xl", "y")
    return jax.shard_map(
        body,
        mesh=parts,
        in_specs=(
            P(ex, mp),
            P(ex, mp),
            P(ex, None),
            P(ex, None),
            P(ex, None),
            P(ex, mp, None),
            P(ex, mp, None),
            P(ex, mp, None),
        ),
        out_specs=(
            P(ex, mp),
            P(ex, None),
            P(ex, mp, None),
            P(ex, mp, None),
            P(ex, mp, None),
        ),
        check_vma=False,
    )
```

```python
import functools

import jax
import jax.numpy as jnp
from jax import lax
from jax.experimental import pallas as pl
from jax.experimental.pallas import tpu as pltpu
from jax.sharding import Mesh
from jax.sharding import PartitionSpec as P

SQRT_TWO_PI = 0.7978845608028654
CUBIC = 0.044715

EXPERTS = 4
CAP = 20
TOK = 32
SHARE = 640
WIDTH = 5120
HID = 160
BLOCK = EXPERTS * CAP
ROWS = 8 * BLOCK
CHIP = 4 * BLOCK
PART = 2 * BLOCK
TALL = PART + 8
XAXES = ("xh", "xl")

BF16 = jnp.bfloat16
F32 = jnp.float32

OFFSET = (0, 1, -1, 2)


def fetch(value, axis, offset, size):
    return lax.ppermute(value, axis, [((i + offset) % size, i) for i in range(size)])


def cross(value, first, offset):
    pairs = []
    for i in range(32):
        xh, core, xl, y = i // 16, i // 8 % 2, i // 4 % 2, i % 4
        x = 2 * xh + xl
        if (core == 0) == first:
            source_x, source_y = (x + offset) % 4, y
        else:
            source_x, source_y = x, (y + offset) % 4
        source = source_x // 2 * 16 + core * 8 + source_x % 2 * 4 + source_y
        pairs.append((source, i))
    return lax.ppermute(value, ("xh", "c", "xl", "y"), pairs)


def pack_kernel(pos_ref, own_ref, other_ref, own_rows, other_rows, *outs):
    core = pos_ref[2]
    row = lax.broadcasted_iota(jnp.int32, (2 * CAP, TOK), 0)
    for k in range(EXPERTS):
        total = jnp.zeros((2 * CAP, SHARE), F32)
        for place, info, rows in ((core, own_ref, own_rows), (1 - core, other_ref, other_rows)):
            values = info[...].astype(F32)
            target, gate = values[0:2], jnp.where(core == 0, 1.0, values[2:4])
            slot = row - place * CAP
            valid = jnp.logical_and(slot >= 0, slot < CAP)
            slot = jnp.where(valid, slot + k * CAP, -2).astype(F32)
            scale = jnp.where(
                target[0:1] == slot,
                gate[0:1],
                jnp.where(target[1:2] == slot, gate[1:2], 0.0),
            ).astype(BF16)
            total = total + jnp.dot(scale, rows[...], preferred_element_type=F32)
        outs[k][...] = total.astype(BF16)


def order_kernel(*refs):
    out = refs[EXPERTS]
    for k in range(EXPERTS):
        block = refs[k][...].astype(F32)
        for group in range(2):
            out[group, k * CAP : (k + 1) * CAP] = block[
                group * CAP : (group + 1) * CAP
            ].astype(BF16)


def combine_kernel(info_ref, *refs):
    blocks, (tok_ref, gates_ref) = refs[:EXPERTS], refs[EXPERTS:]
    info = info_ref[...].astype(F32)
    target = info[0:2]
    slot = lax.broadcasted_iota(jnp.int32, (CAP, TOK), 0).astype(F32)
    every = lax.broadcasted_iota(jnp.int32, (BLOCK, TOK), 0).astype(F32)
    lane = lax.broadcasted_iota(jnp.int32, (1, BLOCK), 1)
    total = jnp.zeros((TOK, SHARE), F32)
    score = jnp.zeros((1, BLOCK), F32)
    for k, block in enumerate(blocks):
        hits = [target[c : c + 1] == slot + k * CAP for c in range(2)]
        one = jnp.where(hits[0], 1.0, jnp.where(hits[1], 1.0, 0.0)).astype(BF16)
        total = total + lax.dot_general(
            one, block[0:CAP], (((0,), (0,)), ((), ())), preferred_element_type=F32
        )
        here = jnp.logical_and(lane >= k * CAP, lane < (k + 1) * CAP)
        score = score + jnp.where(here, block[CAP : CAP + 1, 0:BLOCK].astype(F32), 0.0)
    tok_ref[...] = total.astype(BF16)
    for c in range(2):
        chosen = jnp.where(target[c : c + 1] == every, 1.0, 0.0)
        gates_ref[c : c + 1] = jnp.dot(
            score, chosen, precision=lax.Precision.HIGHEST, preferred_element_type=F32
        ) / info[2 + c : 3 + c]


def stack_kernel(*refs):
    sources, (out, token_ref) = refs[:4], refs[-2:]
    for i in range(4):
        out[i, 0:BLOCK], out[i, BLOCK:PART] = sources[i][0], sources[i][1]
    token_ref[...] = jnp.zeros_like(token_ref)


def copy_kernel(in_ref, after_ref, out_ref):
    del after_ref
    out_ref[...] = in_ref[...]


def join_kernel(token_ref, wg_ref, wu_ref, wd_ref, in_ref, out_ref, sem):
    del token_ref
    copies = [
        pltpu.make_async_copy(wg_ref, in_ref.at[pl.ds(0, HID)], sem.at[0]),
        pltpu.make_async_copy(wu_ref, in_ref.at[pl.ds(HID, HID)], sem.at[1]),
        pltpu.make_async_copy(wd_ref, out_ref, sem.at[2]),
    ]
    for copy in copies:
        copy.start()
    for copy in copies:
        copy.wait()


def place_rows(pos_ref, pieces, by_x_first, place, slots):
    xl = pos_ref[0]
    for last in range(4):
        for inner in range(4):
            ix, iy = (inner, last) if by_x_first else (last, inner)
            slot = place((1 if ix in (1, 2) else 0) * 4 + iy)
            if slot is None:
                continue
            row = (0, xl, 1 - xl, 1)[ix] * CHIP
            if not isinstance(row, int):
                row = pl.multiple_of(row, CHIP)
            slots[slot, pl.ds(row, PART)] = pieces[last][0][inner]
            slots[slot, pl.ds(row + PART, PART)] = pieces[last][1][inner]


def place_both(pos_ref, own, other, x_place, xs, s_place, ss):
    @pl.when(pos_ref[2] == 0)
    def _():
        place_rows(pos_ref, own, True, x_place, xs)
        place_rows(pos_ref, other, False, s_place, ss)

    @pl.when(pos_ref[2] == 1)
    def _():
        place_rows(pos_ref, other, True, x_place, xs)
        place_rows(pos_ref, own, False, s_place, ss)


def columns_of(pos_ref, parity, iy):
    xl, y = pos_ref[0], pos_ref[1]
    offset = jnp.where(iy == 1, 1, jnp.where(iy == 2, 3, jnp.where(iy == 3, 2, 0)))
    block = ((xl + parity) % 2) * 4 + (y + offset) % 4
    return pl.ds(pl.multiple_of(block * SHARE, SHARE), SHARE)


LAST_DIMS = (((1,), (1,)), ((), ()))


def accumulate(pos_ref, acc, w_in, w_out, xs, ss, x_slots, s_slots):
    def x_step(t, carry):
        acc[: 2 * HID] += lax.dot_general(
            w_in[:, columns_of(pos_ref, *x_slots[1](t))],
            xs[t],
            LAST_DIMS,
            preferred_element_type=F32,
        )
        return carry

    def s_step(t, carry):
        acc[2 * HID :] += lax.dot_general(
            w_out[:, columns_of(pos_ref, *s_slots[1](t))],
            ss[t],
            LAST_DIMS,
            preferred_element_type=F32,
        )
        return carry

    lax.fori_loop(0, x_slots[0], x_step, 0)
    lax.fori_loop(0, s_slots[0], s_step, 0)


def early_kernel(pos_ref, w_in, w_out, *refs):
    own, other = [tuple(zip(refs[i : i + 3], refs[i + 3 : i + 6])) for i in (0, 6)]
    acc, xs, ss, token_ref = refs[-4:]
    token_ref[...] = jnp.zeros_like(token_ref)
    place_both(
        pos_ref, own, other,
        lambda j: (j // 4) * 3 + j % 4 if j % 4 < 3 else None, xs,
        lambda j: j - 4 if j >= 4 else None, ss,
    )
    acc[...] = jnp.zeros_like(acc)
    accumulate(
        pos_ref, acc, w_in, w_out, xs, ss,
        (6, lambda t: (t // 3, t % 3)), (4, lambda t: (1, t)),
    )


def late_kernel(pos_ref, w_in, w_out, early_ref, *refs):
    own, other = [
        (refs[i : i + 2], None, None, (refs[i + 2].at[0], refs[i + 2].at[1])) for i in (0, 3)
    ]
    xs, ss, d_ref, h_ref = refs[6:10]
    rows, scores, (acc, all_rows, score_ref) = refs[10:12], refs[12:14], refs[14:]
    place_both(
        pos_ref, own, other,
        lambda j: j // 4 if j % 4 == 3 else None, xs,
        lambda j: j if j < 4 else None, ss,
    )
    acc[...] = early_ref[...]
    accumulate(
        pos_ref, acc, w_in, w_out, xs, ss, (2, lambda t: (t, 3)), (4, lambda t: (0, t))
    )
    pre_gate, pre_up, back = acc[:HID], acc[HID : 2 * HID], acc[2 * HID :]
    tanh_part = jnp.tanh(
        SQRT_TWO_PI * (pre_gate + CUBIC * pre_gate * pre_gate * pre_gate)
    )
    gelu = 0.5 * pre_gate * (1.0 + tanh_part)
    slope = 0.5 * (1.0 + tanh_part) + 0.5 * pre_gate * (
        1.0 - tanh_part * tanh_part
    ) * SQRT_TWO_PI * (1.0 + 3.0 * CUBIC * pre_gate * pre_gate)
    hidden = (gelu * pre_up).astype(BF16)
    h_ref[...] = hidden
    score = jnp.sum(hidden.astype(F32) * back, axis=0, keepdims=True)
    score = jnp.broadcast_to(score, (8, ROWS))
    for b, start in enumerate((0, BLOCK, CHIP, CHIP + BLOCK)):
        turned = score if b == 0 else pltpu.roll(score, ROWS - start, 1)
        score_ref[b] = turned
    d_gate = back * pre_up * slope
    d_up = back * gelu
    d_ref[:HID] = d_gate.astype(BF16)
    d_ref[HID:] = d_up.astype(BF16)
    all_rows[...] = jnp.concatenate([d_gate, d_up], axis=0).T.astype(BF16)
    for i, core in enumerate((pos_ref[2], 1 - pos_ref[2])):
        for b in range(4):
            rows[i][b * BLOCK : (b + 1) * BLOCK] = all_rows[
                pl.ds(pl.multiple_of((2 * b + core) * BLOCK, BLOCK), BLOCK)
            ]
        for x_half in range(2):
            scores[i][x_half] = score_ref[2 * x_half + core]


def rows_kernel(pos_ref, w_own, w_pair, own_rows, pair_rows, own_score, pair_score, out):
    xl, core = pos_ref[0], pos_ref[2]

    def step(j, carry):
        parity, iy = j // 4, j % 4
        columns = columns_of(pos_ref, parity, iy)
        value = jnp.dot(own_rows[...], w_own[:, columns], preferred_element_type=F32)
        value += jnp.dot(pair_rows[...], w_pair[:, columns], preferred_element_type=F32)
        value = value.astype(BF16)
        for x_half in range(2):
            ix = jnp.where(parity == 0, 3 * x_half, 1 + (x_half + xl) % 2)
            first, second = jnp.where(core == 0, ix, iy), jnp.where(core == 0, iy, ix)
            out[first, second, 0:PART] = value[x_half * PART : (x_half + 1) * PART]
            out[first, second, PART:TALL] = (
                own_score[x_half] + pair_score[x_half]
            ).astype(BF16)
        return carry

    lax.fori_loop(0, 8, step, 0)


def weights_kernel(outputs, slots, skip, *refs):
    pos_ref, d_ref, arrays = refs[0], refs[1], refs[2:4]
    refs = refs[4 + skip :]
    outs, token_ref, gs, g_sem = refs[:outputs], *refs[outputs:]
    token_ref[...] = jnp.zeros_like(token_ref)
    done = 0
    for array, (count, features) in zip(arrays, slots):

        def copies(t):
            columns = columns_of(pos_ref, *features(t))
            return [
                pltpu.make_async_copy(
                    gs.at[done + t, pl.ds(i * HID, HID)],
                    outs[i].at[:, columns],
                    g_sem.at[done + t, i],
                )
                for i in range(outputs)
            ]

        def step(t, carry):
            gs[done + t] = jnp.dot(
                d_ref[...], array[t], preferred_element_type=F32
            ).astype(BF16)
            for copy in copies(t):
                copy.start()
            return carry

        lax.fori_loop(0, count, step, 0)
        done += count

    def drain(t, carry):
        for i in range(outputs):
            part = gs.at[t, pl.ds(i * HID, HID)]
            pltpu.make_async_copy(part, part, g_sem.at[t, i]).wait()
        return carry

    lax.fori_loop(0, 8, drain, 0)


def relay_kernel(token, part1, arrival1, part2, arrival2, out1, out2, token_ref):
    del token
    token_ref[...] = jnp.zeros_like(token_ref)
    for t in range(2):
        out1[t] = (part1[t].astype(F32) + arrival1[t].astype(F32)).astype(BF16)
        out2[t] = (part2[t].astype(F32) + arrival2[t].astype(F32)).astype(BF16)


def sum_kernel(token, own, next0, next1, prev0, prev1, *outs):
    del token
    for i, out in enumerate(outs):
        total = own[i].astype(F32)
        total = total + (next0, next1)[i // 2][i % 2].astype(F32)
        total = total + (prev0, prev1)[i // 2][i % 2].astype(F32)
        out[...] = total.astype(BF16)


def homes_kernel(*refs):
    parts, outs = refs[:4], refs[4:6]
    total = (
        parts[0][...].astype(F32)
        + parts[1][...].astype(F32)
        + parts[2][...].astype(F32)
        + parts[3][...].astype(F32)
    )
    scores = total[PART:TALL]
    for z, out in enumerate(outs):
        out[0:BLOCK] = total[z * BLOCK : (z + 1) * BLOCK].astype(BF16)
        if z == 1:
            scores = pltpu.roll(scores, SHARE - PART, 1)
        out[BLOCK : BLOCK + 8] = scores.astype(BF16)


def split_kernel(a_ref, b_ref, *outs):
    total = a_ref[...].astype(F32) + b_ref[...].astype(F32)
    for k, out in enumerate(outs):
        out[0:CAP] = total[k * CAP : (k + 1) * CAP].astype(BF16)
        out[CAP : CAP + 8] = total[BLOCK : BLOCK + 8].astype(BF16)


def pass_kernel(*refs):
    for z in range(2):
        for t in range(4):
            refs[5][z, t] = refs[1 + 2 * z + t // 2][t % 2]


SMEM = pl.BlockSpec(memory_space=pltpu.SMEM)
VMEM = pl.BlockSpec(memory_space=pltpu.VMEM)
ANY = pl.BlockSpec(memory_space=pl.ANY)
HBM = pl.BlockSpec(memory_space=pltpu.HBM)
DMA = pltpu.SemaphoreType.DMA


def shape(dims, dtype=BF16):
    return jax.ShapeDtypeStruct(dims, dtype)


def params(mib):
    return pltpu.CompilerParams(vmem_limit_bytes=mib * 1024 * 1024)


def cost(products, size):
    return pl.CostEstimate(flops=2 * products, bytes_accessed=size, transcendentals=0)


TOKEN = shape((8, 128), F32)


def weights_call(outputs, slots, pos, d, arrays, after):
    return pl.pallas_call(
        functools.partial(weights_kernel, outputs, slots, len(after)),
        out_shape=[shape((HID, WIDTH))] * outputs + [TOKEN],
        in_specs=[SMEM] + [VMEM] * 3 + [ANY] * len(after),
        out_specs=[ANY] * outputs + [VMEM],
        scratch_shapes=[
            pltpu.VMEM((8, outputs * HID, SHARE), BF16),
            DMA((8, outputs)),
        ],
        compiler_params=params(6),
        cost_estimate=cost(
            outputs * HID * ROWS * WIDTH, 2 * WIDTH * (ROWS + outputs * HID)
        ),
    )(pos, d, *arrays, *after)


def scatter(parts, first):
    return [parts[0]] + [cross(parts[i], first, -OFFSET[i]) for i in range(1, 4)]


def between(value, k, dz):
    pairs = [
        ((((e + k) % 4) * 2 + (z ^ dz)), e * 2 + z) for e in range(4) for z in range(2)
    ]
    return lax.ppermute(value, ("e", "zl"), pairs)


def body(tokens, grad_out, expert_ids, slot_ids, gate_weights, gate_proj, up_proj, down_proj):
    core = lax.axis_index("c")
    pos = jnp.stack([lax.axis_index("xl"), lax.axis_index("y"), core]).astype(jnp.int32)
    relative = (expert_ids.T - lax.axis_index("e") + EXPERTS) % EXPERTS
    target = jnp.where(slot_ids.T >= 0, relative * CAP + slot_ids.T, -1)
    info = jnp.concatenate([target.astype(BF16), gate_weights.T], axis=0)
    keep = jnp.where(core == 0, tokens, grad_out)
    give = jnp.where(core == 0, grad_out, tokens)
    packed = pl.pallas_call(
        pack_kernel,
        out_shape=[shape((2 * CAP, SHARE))] * EXPERTS,
        in_specs=[SMEM] + [VMEM] * 4,
        out_specs=[VMEM] * EXPERTS,
        compiler_params=params(2),
    )(pos, info, fetch(info, "c", 1, 2), keep, fetch(give, "c", 1, 2))
    arrived = [packed[0]] + [between(packed[k], -k, 0) for k in range(1, EXPERTS)]
    mine = pl.pallas_call(
        order_kernel,
        out_shape=shape((2, BLOCK, SHARE)),
        in_specs=[VMEM] * EXPERTS,
        out_specs=VMEM,
        compiler_params=params(2),
    )(*arrived)
    theirs = fetch(mine, "zl", 1, 2)
    group, stacks = [mine] + [cross(mine, True, d) for d in OFFSET[1:]], []
    for z in range(2):
        after = () if z else (theirs,)
        stacked, token = pl.pallas_call(
            stack_kernel,
            out_shape=[shape((4, PART, SHARE)), TOKEN],
            in_specs=[VMEM] * 4 + [ANY] * len(after),
            out_specs=[VMEM] * 2,
            compiler_params=params(4),
        )(*group, *after)
        stacks.append(stacked)
        theirs = pl.pallas_call(
            copy_kernel,
            out_shape=shape((2, BLOCK, SHARE)),
            in_specs=[VMEM, ANY],
            out_specs=VMEM,
            compiler_params=params(2),
        )(theirs, group[3])
        if not z:
            group = [theirs] + [cross(theirs, True, d) for d in OFFSET[1:]]
    w_in, w_out = pl.pallas_call(
        join_kernel,
        out_shape=[shape((2 * HID, WIDTH)), shape((HID, WIDTH))],
        in_specs=[VMEM] + [HBM] * 3,
        out_specs=[VMEM] * 2,
        scratch_shapes=[DMA((3,))],
        compiler_params=params(2),
        cost_estimate=cost(0, 12 * HID * WIDTH),
    )(token, gate_proj[0], up_proj[0], down_proj[0])
    w_pair = fetch(w_in, "c", 1, 2)
    own, halves = [], []
    for t in stacks:
        nxt, prev = cross(t, False, 1), cross(t, False, -1)
        own += [t, nxt, prev]
        halves += [cross(prev[:2], False, -1), cross(nxt[2:], False, 1)]
    other = [fetch(t, "c", 1, 2) for t in own]
    early, xs_early, ss_early, token = pl.pallas_call(
        early_kernel,
        out_shape=[
            shape((3 * HID, ROWS), F32),
            shape((6, ROWS, SHARE)),
            shape((4, ROWS, SHARE)),
            TOKEN,
        ],
        in_specs=[SMEM] + [VMEM] * 14,
        out_specs=[VMEM] * 4,
        compiler_params=params(4),
        cost_estimate=cost(0, 0),
    )(pos, w_in, w_out, *own, *other)
    last = pl.pallas_call(
        pass_kernel,
        out_shape=shape((2, 4, PART, SHARE)),
        in_specs=[ANY] + [VMEM] * 4,
        out_specs=VMEM,
        compiler_params=params(4),
    )(token, *halves)
    half_rows, half_score = shape((ROWS // 2, 2 * HID)), shape((2, 8, ROWS), F32)
    xs_late, ss_late, d, hidden, rows, pair_rows, score, pair_score = pl.pallas_call(
        late_kernel,
        out_shape=[
            shape((2, ROWS, SHARE)),
            shape((4, ROWS, SHARE)),
            shape((2 * HID, ROWS)),
            shape((HID, ROWS)),
            half_rows,
            half_rows,
            half_score,
            half_score,
        ],
        in_specs=[SMEM] + [VMEM] * 9,
        out_specs=[VMEM] * 8,
        scratch_shapes=[
            pltpu.VMEM((3 * HID, ROWS), F32),
            pltpu.VMEM((ROWS, 2 * HID), BF16),
            pltpu.VMEM((4, 8, ROWS), F32),
        ],
        compiler_params=params(10),
        cost_estimate=cost(
            HID * ROWS * WIDTH, 2 * WIDTH * (3 * HID + ROWS * 3 // 4)
        ),
    )(
        pos, w_in, w_out, early, *stacks, last, other[0], other[3], fetch(last, "c", 1, 2)
    )
    sums = pl.pallas_call(
        rows_kernel,
        out_shape=shape((4, 4, TALL, SHARE)),
        in_specs=[SMEM] + [VMEM] * 6,
        out_specs=VMEM,
        compiler_params=params(4),
        cost_estimate=cost(
            2 * HID * ROWS * WIDTH, 2 * WIDTH * (ROWS // 2 + 4 * HID)
        ),
    )(
        pos, w_in, w_pair, rows, fetch(pair_rows, "c", 1, 2), score, fetch(pair_score, "c", 1, 2)
    )
    part = sums[0]
    halves = [[sums[i, t : t + 2] for t in (0, 2)] for i in range(1, 4)]
    arrivals = [cross(halves[2][0], True, -1), cross(halves[2][1], True, 1)]
    from_prev, from_next = cross(halves[0][1], True, -1), cross(halves[1][0], True, 1)
    grad_down, token = weights_call(
        1, ((4, lambda t: (1, t)), (4, lambda t: (0, t))), pos, hidden, (ss_early, ss_late),
        (halves[2][0],),
    )
    to_next, to_prev, token = pl.pallas_call(
        relay_kernel,
        out_shape=[shape((2, TALL, SHARE))] * 2 + [TOKEN],
        in_specs=[ANY] + [VMEM] * 4,
        out_specs=[VMEM] * 3,
        compiler_params=params(4),
    )(token, halves[0][0], arrivals[0], halves[1][1], arrivals[1])
    grad_gate, grad_up, token = weights_call(
        2, ((6, lambda t: (t // 3, t % 3)), (2, lambda t: (t, 3))), pos, d, (xs_early, xs_late),
        (token,),
    )
    parts = pl.pallas_call(
        sum_kernel,
        out_shape=[shape((TALL, SHARE))] * 4,
        in_specs=[ANY] + [VMEM] * 5,
        out_specs=[VMEM] * 4,
        compiler_params=params(4),
    )(
        token, part, cross(to_next, True, -1), from_prev, from_next, cross(to_prev, True, 1)
    )
    here, there = pl.pallas_call(
        homes_kernel,
        out_shape=[shape((BLOCK + 8, SHARE))] * 2,
        in_specs=[VMEM] * 4,
        out_specs=[VMEM] * 2,
        compiler_params=params(4),
    )(*scatter(parts, False))
    blocks = pl.pallas_call(
        split_kernel,
        out_shape=[shape((CAP + 8, SHARE))] * EXPERTS,
        in_specs=[VMEM] * 2,
        out_specs=[VMEM] * EXPERTS,
        compiler_params=params(4),
    )(here, fetch(there, "zl", 1, 2))
    blocks = [blocks[0]] + [between(blocks[k], k, 0) for k in range(1, EXPERTS)]

    grad_tokens, grad_gates = pl.pallas_call(
        combine_kernel,
        out_shape=[shape((TOK, SHARE)), shape((2, TOK), F32)],
        in_specs=[VMEM] * 5,
        out_specs=[VMEM] * 2,
        compiler_params=params(4),
    )(info, *blocks)
    return (grad_tokens, grad_gates.T, grad_gate[None], grad_up[None], grad_down[None])


def solution(mesh):
    parts = Mesh(
        mesh.devices.reshape(4, 2, 2, 2, 2, 4), ("e", "zl", "xh", "c", "xl", "y")
    )
    ex, mp = ("e", "zl", "xh", "c"), ("xl", "y")
    return jax.shard_map(
        body,
        mesh=parts,
        in_specs=(
            P(ex, mp),
            P(ex, mp),
            P(ex, None),
            P(ex, None),
            P(ex, None),
            P(ex, mp, None),
            P(ex, mp, None),
            P(ex, mp, None),
        ),
        out_specs=(
            P(ex, mp),
            P(ex, None),
            P(ex, mp, None),
            P(ex, mp, None),
            P(ex, mp, None),
        ),
        check_vma=False,
    )
```

```python
import functools

import jax
import jax.numpy as jnp
from jax import lax
from jax.experimental import pallas as pl
from jax.experimental.pallas import tpu as pltpu
from jax.sharding import Mesh
from jax.sharding import PartitionSpec as P

SQRT_TWO_PI = 0.7978845608028654
CUBIC = 0.044715

EXPERTS = 4
ORDER = (2, 1, 3, 0)
CAP = 20
TOK = 32
SHARE = 640
WIDTH = 5120
HID = 160
BLOCK = EXPERTS * CAP
ROWS = 8 * BLOCK
CHIP = 4 * BLOCK
PART = 2 * BLOCK
TALL = PART + 8
XAXES = ("xh", "xl")

BF16 = jnp.bfloat16
F32 = jnp.float32

OFFSET = (0, 1, -1, 2)


def fetch(value, axis, offset, size):
    return lax.ppermute(value, axis, [((i + offset) % size, i) for i in range(size)])


def cross(value, first, offset):
    pairs = []
    for i in range(32):
        xh, core, xl, y = i // 16, i // 8 % 2, i // 4 % 2, i % 4
        x = 2 * xh + xl
        if (core == 0) == first:
            source_x, source_y = (x + offset) % 4, y
        else:
            source_x, source_y = x, (y + offset) % 4
        source = source_x // 2 * 16 + core * 8 + source_x % 2 * 4 + source_y
        pairs.append((source, i))
    return lax.ppermute(value, ("xh", "c", "xl", "y"), pairs)


def pack_kernel(pos_ref, own_ref, other_ref, own_rows, other_rows, *outs):
    core = pos_ref[2]
    row = lax.broadcasted_iota(jnp.int32, (2 * CAP, TOK), 0)
    for k in range(EXPERTS):
        total = jnp.zeros((2 * CAP, SHARE), F32)
        for place, info, rows in ((core, own_ref, own_rows), (1 - core, other_ref, other_rows)):
            values = info[...].astype(F32)
            target, gate = values[0:2], jnp.where(core == 0, 1.0, values[2:4])
            slot = row - place * CAP
            valid = jnp.logical_and(slot >= 0, slot < CAP)
            slot = jnp.where(valid, slot + k * CAP, -2).astype(F32)
            scale = jnp.where(
                target[0:1] == slot,
                gate[0:1],
                jnp.where(target[1:2] == slot, gate[1:2], 0.0),
            ).astype(BF16)
            total = total + jnp.dot(scale, rows[...], preferred_element_type=F32)
        outs[k][...] = total.astype(BF16)


def order_kernel(*refs):
    out = refs[EXPERTS]
    for i, k in enumerate(ORDER):
        block = refs[i][...].astype(F32)
        for group in range(2):
            out[group, k * CAP : (k + 1) * CAP] = block[
                group * CAP : (group + 1) * CAP
            ].astype(BF16)


def combine_kernel(info_ref, *refs):
    blocks, (tok_ref, gates_ref) = refs[:EXPERTS], refs[EXPERTS:]
    info = info_ref[...].astype(F32)
    target = info[0:2]
    slot = lax.broadcasted_iota(jnp.int32, (CAP, TOK), 0).astype(F32)
    every = lax.broadcasted_iota(jnp.int32, (BLOCK, TOK), 0).astype(F32)
    lane = lax.broadcasted_iota(jnp.int32, (1, BLOCK), 1)
    total = jnp.zeros((TOK, SHARE), F32)
    score = jnp.zeros((1, BLOCK), F32)
    for k, block in zip(ORDER, blocks):
        hits = [target[c : c + 1] == slot + k * CAP for c in range(2)]
        one = jnp.where(hits[0], 1.0, jnp.where(hits[1], 1.0, 0.0)).astype(BF16)
        total = total + lax.dot_general(
            one, block[0:CAP], (((0,), (0,)), ((), ())), preferred_element_type=F32
        )
        here = jnp.logical_and(lane >= k * CAP, lane < (k + 1) * CAP)
        score = score + jnp.where(here, block[CAP : CAP + 1, 0:BLOCK].astype(F32), 0.0)
    tok_ref[...] = total.astype(BF16)
    for c in range(2):
        chosen = jnp.where(target[c : c + 1] == every, 1.0, 0.0)
        gates_ref[c : c + 1] = jnp.dot(
            score, chosen, precision=lax.Precision.HIGHEST, preferred_element_type=F32
        ) / info[2 + c : 3 + c]


def stack_kernel(*refs):
    sources, (out, token_ref) = refs[:4], refs[-2:]
    for i in range(4):
        out[i, 0:BLOCK], out[i, BLOCK:PART] = sources[i][0], sources[i][1]
    token_ref[...] = jnp.zeros_like(token_ref)


def copy_kernel(in_ref, after_ref, out_ref):
    del after_ref
    out_ref[...] = in_ref[...]


def join_kernel(token_ref, wg_ref, wu_ref, wd_ref, in_ref, out_ref, sem):
    del token_ref
    copies = [
        pltpu.make_async_copy(wg_ref, in_ref.at[pl.ds(0, HID)], sem.at[0]),
        pltpu.make_async_copy(wu_ref, in_ref.at[pl.ds(HID, HID)], sem.at[1]),
        pltpu.make_async_copy(wd_ref, out_ref, sem.at[2]),
    ]
    for copy in copies:
        copy.start()
    for copy in copies:
        copy.wait()


def place_rows(pos_ref, pieces, by_x_first, place, slots):
    xl = pos_ref[0]
    for last in range(4):
        for inner in range(4):
            ix, iy = (inner, last) if by_x_first else (last, inner)
            slot = place((1 if ix in (1, 2) else 0) * 4 + iy)
            if slot is None:
                continue
            row = (0, xl, 1 - xl, 1)[ix] * CHIP
            if not isinstance(row, int):
                row = pl.multiple_of(row, CHIP)
            slots[slot, pl.ds(row, PART)] = pieces[last][0][inner]
            slots[slot, pl.ds(row + PART, PART)] = pieces[last][1][inner]


def place_both(pos_ref, own, other, x_place, xs, s_place, ss):
    @pl.when(pos_ref[2] == 0)
    def _():
        place_rows(pos_ref, own, True, x_place, xs)
        place_rows(pos_ref, other, False, s_place, ss)

    @pl.when(pos_ref[2] == 1)
    def _():
        place_rows(pos_ref, other, True, x_place, xs)
        place_rows(pos_ref, own, False, s_place, ss)


def columns_of(pos_ref, parity, iy):
    xl, y = pos_ref[0], pos_ref[1]
    offset = jnp.where(iy == 1, 1, jnp.where(iy == 2, 3, jnp.where(iy == 3, 2, 0)))
    block = ((xl + parity) % 2) * 4 + (y + offset) % 4
    return pl.ds(pl.multiple_of(block * SHARE, SHARE), SHARE)


LAST_DIMS = (((1,), (1,)), ((), ()))


def accumulate(pos_ref, acc, w_in, w_out, xs, ss, x_slots, s_slots):
    def x_step(t, carry):
        acc[: 2 * HID] += lax.dot_general(
            w_in[:, columns_of(pos_ref, *x_slots[1](t))],
            xs[t],
            LAST_DIMS,
            preferred_element_type=F32,
        )
        return carry

    def s_step(t, carry):
        acc[2 * HID :] += lax.dot_general(
            w_out[:, columns_of(pos_ref, *s_slots[1](t))],
            ss[t],
            LAST_DIMS,
            preferred_element_type=F32,
        )
        return carry

    lax.fori_loop(0, x_slots[0], x_step, 0)
    lax.fori_loop(0, s_slots[0], s_step, 0)


def early_kernel(pos_ref, w_in, w_out, *refs):
    own, other = [tuple(zip(refs[i : i + 3], refs[i + 3 : i + 6])) for i in (0, 6)]
    acc, xs, ss, token_ref = refs[-4:]
    token_ref[...] = jnp.zeros_like(token_ref)
    place_both(
        pos_ref, own, other,
        lambda j: (j // 4) * 3 + j % 4 if j % 4 < 3 else None, xs,
        lambda j: j - 4 if j >= 4 else None, ss,
    )
    acc[...] = jnp.zeros_like(acc)
    accumulate(
        pos_ref, acc, w_in, w_out, xs, ss,
        (6, lambda t: (t // 3, t % 3)), (4, lambda t: (1, t)),
    )


def late_kernel(pos_ref, w_in, w_out, early_ref, *refs):
    own, other = [
        (refs[i : i + 2], None, None, (refs[i + 2].at[0], refs[i + 2].at[1])) for i in (0, 3)
    ]
    xs, ss, d_ref, h_ref = refs[6:10]
    rows, scores, (acc, all_rows, score_ref) = refs[10:12], refs[12:14], refs[14:]
    place_both(
        pos_ref, own, other,
        lambda j: j // 4 if j % 4 == 3 else None, xs,
        lambda j: j if j < 4 else None, ss,
    )
    acc[...] = early_ref[...]
    accumulate(
        pos_ref, acc, w_in, w_out, xs, ss, (2, lambda t: (t, 3)), (4, lambda t: (0, t))
    )
    pre_gate, pre_up, back = acc[:HID], acc[HID : 2 * HID], acc[2 * HID :]
    tanh_part = jnp.tanh(
        SQRT_TWO_PI * (pre_gate + CUBIC * pre_gate * pre_gate * pre_gate)
    )
    gelu = 0.5 * pre_gate * (1.0 + tanh_part)
    slope = 0.5 * (1.0 + tanh_part) + 0.5 * pre_gate * (
        1.0 - tanh_part * tanh_part
    ) * SQRT_TWO_PI * (1.0 + 3.0 * CUBIC * pre_gate * pre_gate)
    hidden = (gelu * pre_up).astype(BF16)
    h_ref[...] = hidden
    score = jnp.sum(hidden.astype(F32) * back, axis=0, keepdims=True)
    score = jnp.broadcast_to(score, (8, ROWS))
    for b, start in enumerate((0, BLOCK, CHIP, CHIP + BLOCK)):
        turned = score if b == 0 else pltpu.roll(score, ROWS - start, 1)
        score_ref[b] = turned
    d_gate = back * pre_up * slope
    d_up = back * gelu
    d_ref[:HID] = d_gate.astype(BF16)
    d_ref[HID:] = d_up.astype(BF16)
    all_rows[...] = jnp.concatenate([d_gate, d_up], axis=0).T.astype(BF16)
    for i, core in enumerate((pos_ref[2], 1 - pos_ref[2])):
        for b in range(4):
            rows[i][b * BLOCK : (b + 1) * BLOCK] = all_rows[
                pl.ds(pl.multiple_of((2 * b + core) * BLOCK, BLOCK), BLOCK)
            ]
        for x_half in range(2):
            scores[i][x_half] = score_ref[2 * x_half + core]


def rows_kernel(pos_ref, w_own, w_pair, own_rows, pair_rows, own_score, pair_score, out):
    xl, core = pos_ref[0], pos_ref[2]

    def step(j, carry):
        parity, iy = j // 4, j % 4
        columns = columns_of(pos_ref, parity, iy)
        value = jnp.dot(own_rows[...], w_own[:, columns], preferred_element_type=F32)
        value += jnp.dot(pair_rows[...], w_pair[:, columns], preferred_element_type=F32)
        value = value.astype(BF16)
        for x_half in range(2):
            ix = jnp.where(parity == 0, 3 * x_half, 1 + (x_half + xl) % 2)
            first, second = jnp.where(core == 0, ix, iy), jnp.where(core == 0, iy, ix)
            out[first, second, 0:PART] = value[x_half * PART : (x_half + 1) * PART]
            out[first, second, PART:TALL] = (
                own_score[x_half] + pair_score[x_half]
            ).astype(BF16)
        return carry

    lax.fori_loop(0, 8, step, 0)


def weights_kernel(outputs, slots, skip, *refs):
    pos_ref, d_ref, arrays = refs[0], refs[1], refs[2:4]
    refs = refs[4 + skip :]
    outs, token_ref, gs, g_sem = refs[:outputs], *refs[outputs:]
    token_ref[...] = jnp.zeros_like(token_ref)
    done = 0
    for array, (count, features) in zip(arrays, slots):

        def copies(t):
            columns = columns_of(pos_ref, *features(t))
            return [
                pltpu.make_async_copy(
                    gs.at[done + t, pl.ds(i * HID, HID)],
                    outs[i].at[:, columns],
                    g_sem.at[done + t, i],
                )
                for i in range(outputs)
            ]

        def step(t, carry):
            gs[done + t] = jnp.dot(
                d_ref[...], array[t], preferred_element_type=F32
            ).astype(BF16)
            for copy in copies(t):
                copy.start()
            return carry

        lax.fori_loop(0, count, step, 0)
        done += count

    def drain(t, carry):
        for i in range(outputs):
            part = gs.at[t, pl.ds(i * HID, HID)]
            pltpu.make_async_copy(part, part, g_sem.at[t, i]).wait()
        return carry

    lax.fori_loop(0, 8, drain, 0)


def relay_kernel(token, part1, arrival1, part2, arrival2, out1, out2, token_ref):
    del token
    token_ref[...] = jnp.zeros_like(token_ref)
    for t in range(2):
        out1[t] = (part1[t].astype(F32) + arrival1[t].astype(F32)).astype(BF16)
        out2[t] = (part2[t].astype(F32) + arrival2[t].astype(F32)).astype(BF16)


def sum_kernel(token, own, next0, next1, prev0, prev1, *outs):
    del token
    for i, out in enumerate(outs):
        total = own[i].astype(F32)
        total = total + (next0, next1)[i // 2][i % 2].astype(F32)
        total = total + (prev0, prev1)[i // 2][i % 2].astype(F32)
        out[...] = total.astype(BF16)


def homes_kernel(*refs):
    parts, outs = refs[:4], refs[4:6]
    total = (
        parts[0][...].astype(F32)
        + parts[1][...].astype(F32)
        + parts[2][...].astype(F32)
        + parts[3][...].astype(F32)
    )
    scores = total[PART:TALL]
    for z, out in enumerate(outs):
        out[0:BLOCK] = total[z * BLOCK : (z + 1) * BLOCK].astype(BF16)
        if z == 1:
            scores = pltpu.roll(scores, SHARE - PART, 1)
        out[BLOCK : BLOCK + 8] = scores.astype(BF16)


def split_kernel(a_ref, b_ref, *outs):
    total = a_ref[...].astype(F32) + b_ref[...].astype(F32)
    for k, out in enumerate(outs):
        out[0:CAP] = total[k * CAP : (k + 1) * CAP].astype(BF16)
        out[CAP : CAP + 8] = total[BLOCK : BLOCK + 8].astype(BF16)


def pass_kernel(*refs):
    for z in range(2):
        for t in range(4):
            refs[5][z, t] = refs[1 + 2 * z + t // 2][t % 2]


SMEM = pl.BlockSpec(memory_space=pltpu.SMEM)
VMEM = pl.BlockSpec(memory_space=pltpu.VMEM)
ANY = pl.BlockSpec(memory_space=pl.ANY)
HBM = pl.BlockSpec(memory_space=pltpu.HBM)
DMA = pltpu.SemaphoreType.DMA


def shape(dims, dtype=BF16):
    return jax.ShapeDtypeStruct(dims, dtype)


def params(mib):
    return pltpu.CompilerParams(vmem_limit_bytes=mib * 1024 * 1024)


def cost(products, size):
    return pl.CostEstimate(flops=2 * products, bytes_accessed=size, transcendentals=0)


TOKEN = shape((8, 128), F32)


def weights_call(outputs, slots, pos, d, arrays, after):
    return pl.pallas_call(
        functools.partial(weights_kernel, outputs, slots, len(after)),
        out_shape=[shape((HID, WIDTH))] * outputs + [TOKEN],
        in_specs=[SMEM] + [VMEM] * 3 + [ANY] * len(after),
        out_specs=[ANY] * outputs + [VMEM],
        scratch_shapes=[
            pltpu.VMEM((8, outputs * HID, SHARE), BF16),
            DMA((8, outputs)),
        ],
        compiler_params=params(6),
        cost_estimate=cost(
            outputs * HID * ROWS * WIDTH, 2 * WIDTH * (ROWS + outputs * HID)
        ),
    )(pos, d, *arrays, *after)


def scatter(parts, first):
    return [cross(parts[i], first, -OFFSET[i]) for i in (3, 1, 2)] + [parts[0]]


def between(value, k, dz):
    pairs = [
        ((((e + k) % 4) * 2 + (z ^ dz)), e * 2 + z) for e in range(4) for z in range(2)
    ]
    return lax.ppermute(value, ("e", "zl"), pairs)


def body(tokens, grad_out, expert_ids, slot_ids, gate_weights, gate_proj, up_proj, down_proj):
    core = lax.axis_index("c")
    pos = jnp.stack([lax.axis_index("xl"), lax.axis_index("y"), core]).astype(jnp.int32)
    relative = (expert_ids.T - lax.axis_index("e") + EXPERTS) % EXPERTS
    target = jnp.where(slot_ids.T >= 0, relative * CAP + slot_ids.T, -1)
    info = jnp.concatenate([target.astype(BF16), gate_weights.T], axis=0)
    keep = jnp.where(core == 0, tokens, grad_out)
    give = jnp.where(core == 0, grad_out, tokens)
    packed = pl.pallas_call(
        pack_kernel,
        out_shape=[shape((2 * CAP, SHARE))] * EXPERTS,
        in_specs=[SMEM] + [VMEM] * 4,
        out_specs=[VMEM] * EXPERTS,
        compiler_params=params(2),
    )(pos, info, fetch(info, "c", 1, 2), keep, fetch(give, "c", 1, 2))
    arrived = [between(packed[k], -k, 0) for k in ORDER[:3]] + [packed[0]]
    mine = pl.pallas_call(
        order_kernel,
        out_shape=shape((2, BLOCK, SHARE)),
        in_specs=[VMEM] * EXPERTS,
        out_specs=VMEM,
        compiler_params=params(2),
    )(*arrived)
    theirs = fetch(mine, "zl", 1, 2)
    group, stacks = [mine] + [cross(mine, True, d) for d in OFFSET[1:]], []
    for z in range(2):
        after = () if z else (theirs,)
        stacked, token = pl.pallas_call(
            stack_kernel,
            out_shape=[shape((4, PART, SHARE)), TOKEN],
            in_specs=[VMEM] * 4 + [ANY] * len(after),
            out_specs=[VMEM] * 2,
            compiler_params=params(4),
        )(*group, *after)
        stacks.append(stacked)
        theirs = pl.pallas_call(
            copy_kernel,
            out_shape=shape((2, BLOCK, SHARE)),
            in_specs=[VMEM, ANY],
            out_specs=VMEM,
            compiler_params=params(2),
        )(theirs, group[3])
        if not z:
            group = [theirs] + [cross(theirs, True, d) for d in OFFSET[1:]]
    w_in, w_out = pl.pallas_call(
        join_kernel,
        out_shape=[shape((2 * HID, WIDTH)), shape((HID, WIDTH))],
        in_specs=[VMEM] + [HBM] * 3,
        out_specs=[VMEM] * 2,
        scratch_shapes=[DMA((3,))],
        compiler_params=params(2),
        cost_estimate=cost(0, 12 * HID * WIDTH),
    )(token, gate_proj[0], up_proj[0], down_proj[0])
    w_pair = fetch(w_in, "c", 1, 2)
    own, halves = [], []
    for t in stacks:
        nxt, prev = cross(t, False, 1), cross(t, False, -1)
        own += [t, nxt, prev]
        halves += [cross(prev[:2], False, -1), cross(nxt[2:], False, 1)]
    other = [fetch(t, "c", 1, 2) for t in own]
    early, xs_early, ss_early, token = pl.pallas_call(
        early_kernel,
        out_shape=[
            shape((3 * HID, ROWS), F32),
            shape((6, ROWS, SHARE)),
            shape((4, ROWS, SHARE)),
            TOKEN,
        ],
        in_specs=[SMEM] + [VMEM] * 14,
        out_specs=[VMEM] * 4,
        compiler_params=params(4),
        cost_estimate=cost(0, 0),
    )(pos, w_in, w_out, *own, *other)
    last = pl.pallas_call(
        pass_kernel,
        out_shape=shape((2, 4, PART, SHARE)),
        in_specs=[ANY] + [VMEM] * 4,
        out_specs=VMEM,
        compiler_params=params(4),
    )(token, *halves)
    half_rows, half_score = shape((ROWS // 2, 2 * HID)), shape((2, 8, ROWS), F32)
    xs_late, ss_late, d, hidden, rows, pair_rows, score, pair_score = pl.pallas_call(
        late_kernel,
        out_shape=[
            shape((2, ROWS, SHARE)),
            shape((4, ROWS, SHARE)),
            shape((2 * HID, ROWS)),
            shape((HID, ROWS)),
            half_rows,
            half_rows,
            half_score,
            half_score,
        ],
        in_specs=[SMEM] + [VMEM] * 9,
        out_specs=[VMEM] * 8,
        scratch_shapes=[
            pltpu.VMEM((3 * HID, ROWS), F32),
            pltpu.VMEM((ROWS, 2 * HID), BF16),
            pltpu.VMEM((4, 8, ROWS), F32),
        ],
        compiler_params=params(10),
        cost_estimate=cost(
            HID * ROWS * WIDTH, 2 * WIDTH * (3 * HID + ROWS * 3 // 4)
        ),
    )(
        pos, w_in, w_out, early, *stacks, last, other[0], other[3], fetch(last, "c", 1, 2)
    )
    sums = pl.pallas_call(
        rows_kernel,
        out_shape=shape((4, 4, TALL, SHARE)),
        in_specs=[SMEM] + [VMEM] * 6,
        out_specs=VMEM,
        compiler_params=params(4),
        cost_estimate=cost(
            2 * HID * ROWS * WIDTH, 2 * WIDTH * (ROWS // 2 + 4 * HID)
        ),
    )(
        pos, w_in, w_pair, rows, fetch(pair_rows, "c", 1, 2), score, fetch(pair_score, "c", 1, 2)
    )
    part = sums[0]
    halves = [[sums[i, t : t + 2] for t in (0, 2)] for i in range(1, 4)]
    arrivals = [cross(halves[2][0], True, -1), cross(halves[2][1], True, 1)]
    from_prev, from_next = cross(halves[0][1], True, -1), cross(halves[1][0], True, 1)
    grad_down, token = weights_call(
        1, ((4, lambda t: (1, t)), (4, lambda t: (0, t))), pos, hidden, (ss_early, ss_late),
        (halves[2][0],),
    )
    to_next, to_prev, token = pl.pallas_call(
        relay_kernel,
        out_shape=[shape((2, TALL, SHARE))] * 2 + [TOKEN],
        in_specs=[ANY] + [VMEM] * 4,
        out_specs=[VMEM] * 3,
        compiler_params=params(4),
    )(token, halves[0][0], arrivals[0], halves[1][1], arrivals[1])
    grad_gate, grad_up, token = weights_call(
        2, ((6, lambda t: (t // 3, t % 3)), (2, lambda t: (t, 3))), pos, d, (xs_early, xs_late),
        (token,),
    )
    parts = pl.pallas_call(
        sum_kernel,
        out_shape=[shape((TALL, SHARE))] * 4,
        in_specs=[ANY] + [VMEM] * 5,
        out_specs=[VMEM] * 4,
        compiler_params=params(4),
    )(
        token, part, cross(to_next, True, -1), from_prev, from_next, cross(to_prev, True, 1)
    )
    here, there = pl.pallas_call(
        homes_kernel,
        out_shape=[shape((BLOCK + 8, SHARE))] * 2,
        in_specs=[VMEM] * 4,
        out_specs=[VMEM] * 2,
        compiler_params=params(4),
    )(*scatter(parts, False))
    blocks = pl.pallas_call(
        split_kernel,
        out_shape=[shape((CAP + 8, SHARE))] * EXPERTS,
        in_specs=[VMEM] * 2,
        out_specs=[VMEM] * EXPERTS,
        compiler_params=params(4),
    )(here, fetch(there, "zl", 1, 2))
    blocks = [between(blocks[k], k, 0) for k in ORDER[:3]] + [blocks[0]]

    grad_tokens, grad_gates = pl.pallas_call(
        combine_kernel,
        out_shape=[shape((TOK, SHARE)), shape((2, TOK), F32)],
        in_specs=[VMEM] * 5,
        out_specs=[VMEM] * 2,
        compiler_params=params(4),
    )(info, *blocks)
    return (grad_tokens, grad_gates.T, grad_gate[None], grad_up[None], grad_down[None])


def solution(mesh):
    parts = Mesh(
        mesh.devices.reshape(4, 2, 2, 2, 2, 4), ("e", "zl", "xh", "c", "xl", "y")
    )
    ex, mp = ("e", "zl", "xh", "c"), ("xl", "y")
    return jax.shard_map(
        body,
        mesh=parts,
        in_specs=(
            P(ex, mp),
            P(ex, mp),
            P(ex, None),
            P(ex, None),
            P(ex, None),
            P(ex, mp, None),
            P(ex, mp, None),
            P(ex, mp, None),
        ),
        out_specs=(
            P(ex, mp),
            P(ex, None),
            P(ex, mp, None),
            P(ex, mp, None),
            P(ex, mp, None),
        ),
        check_vma=False,
    )
```

```python
import functools

import jax
import jax.numpy as jnp
from jax import lax
from jax.experimental import pallas as pl
from jax.experimental.pallas import tpu as pltpu
from jax.sharding import Mesh
from jax.sharding import PartitionSpec as P

SQRT_TWO_PI = 0.7978845608028654
CUBIC = 0.044715

EXPERTS = 4
ORDER = (2, 1, 3, 0)
CAP = 20
TOK = 32
SHARE = 640
WIDTH = 5120
HID = 160
BLOCK = EXPERTS * CAP
ROWS = 8 * BLOCK
CHIP = 4 * BLOCK
PART = 2 * BLOCK
TALL = PART + 8
XAXES = ("xh", "xl")

BF16 = jnp.bfloat16
F32 = jnp.float32

OFFSET = (0, 1, -1, 2)


def fetch(value, axis, offset, size):
    return lax.ppermute(value, axis, [((i + offset) % size, i) for i in range(size)])


def cross(value, first, offset):
    pairs = []
    for i in range(32):
        xh, core, xl, y = i // 16, i // 8 % 2, i // 4 % 2, i % 4
        x = 2 * xh + xl
        if (core == 0) == first:
            source_x, source_y = (x + offset) % 4, y
        else:
            source_x, source_y = x, (y + offset) % 4
        source = source_x // 2 * 16 + core * 8 + source_x % 2 * 4 + source_y
        pairs.append((source, i))
    return lax.ppermute(value, ("xh", "c", "xl", "y"), pairs)


def pack_kernel(pos_ref, own_ref, other_ref, own_rows, other_rows, *outs):
    core = pos_ref[2]
    row = lax.broadcasted_iota(jnp.int32, (2 * CAP, TOK), 0)
    for k in range(EXPERTS):
        total = jnp.zeros((2 * CAP, SHARE), F32)
        for place, info, rows in ((core, own_ref, own_rows), (1 - core, other_ref, other_rows)):
            values = info[...].astype(F32)
            target, gate = values[0:2], jnp.where(core == 0, 1.0, values[2:4])
            slot = row - place * CAP
            valid = jnp.logical_and(slot >= 0, slot < CAP)
            slot = jnp.where(valid, slot + k * CAP, -2).astype(F32)
            scale = jnp.where(
                target[0:1] == slot,
                gate[0:1],
                jnp.where(target[1:2] == slot, gate[1:2], 0.0),
            ).astype(BF16)
            total = total + jnp.dot(scale, rows[...], preferred_element_type=F32)
        outs[k][...] = total.astype(BF16)


def order_kernel(*refs):
    out = refs[EXPERTS]
    for i, k in enumerate(ORDER):
        block = refs[i][...].astype(F32)
        for group in range(2):
            out[group, k * CAP : (k + 1) * CAP] = block[
                group * CAP : (group + 1) * CAP
            ].astype(BF16)


def combine_kernel(info_ref, *refs):
    blocks, (tok_ref, gates_ref) = refs[:EXPERTS], refs[EXPERTS:]
    info = info_ref[...].astype(F32)
    target = info[0:2]
    slot = lax.broadcasted_iota(jnp.int32, (CAP, TOK), 0).astype(F32)
    every = lax.broadcasted_iota(jnp.int32, (BLOCK, TOK), 0).astype(F32)
    lane = lax.broadcasted_iota(jnp.int32, (1, BLOCK), 1)
    total = jnp.zeros((TOK, SHARE), F32)
    score = jnp.zeros((1, BLOCK), F32)
    for k, block in zip(ORDER, blocks):
        hits = [target[c : c + 1] == slot + k * CAP for c in range(2)]
        one = jnp.where(hits[0], 1.0, jnp.where(hits[1], 1.0, 0.0)).astype(BF16)
        total = total + lax.dot_general(
            one, block[0:CAP], (((0,), (0,)), ((), ())), preferred_element_type=F32
        )
        here = jnp.logical_and(lane >= k * CAP, lane < (k + 1) * CAP)
        score = score + jnp.where(here, block[CAP : CAP + 1, 0:BLOCK].astype(F32), 0.0)
    tok_ref[...] = total.astype(BF16)
    for c in range(2):
        chosen = jnp.where(target[c : c + 1] == every, 1.0, 0.0)
        gates_ref[c : c + 1] = jnp.dot(
            score, chosen, precision=lax.Precision.HIGHEST, preferred_element_type=F32
        ) / info[2 + c : 3 + c]


def stack_kernel(*refs):
    sources, (out, token_ref) = refs[:4], refs[-2:]
    for i, source in zip((3, 1, 2, 0), sources):
        out[i, 0:BLOCK], out[i, BLOCK:PART] = source[0], source[1]
    token_ref[...] = jnp.zeros_like(token_ref)


def copy_kernel(in_ref, after_ref, out_ref):
    del after_ref
    out_ref[...] = in_ref[...]


def join_kernel(token_ref, wg_ref, wu_ref, wd_ref, in_ref, out_ref, sem):
    del token_ref
    copies = [
        pltpu.make_async_copy(wg_ref, in_ref.at[pl.ds(0, HID)], sem.at[0]),
        pltpu.make_async_copy(wu_ref, in_ref.at[pl.ds(HID, HID)], sem.at[1]),
        pltpu.make_async_copy(wd_ref, out_ref, sem.at[2]),
    ]
    for copy in copies:
        copy.start()
    for copy in copies:
        copy.wait()


def place_rows(pos_ref, pieces, by_x_first, place, slots):
    xl = pos_ref[0]
    for last in range(4):
        for inner in range(4):
            ix, iy = (inner, last) if by_x_first else (last, inner)
            slot = place((1 if ix in (1, 2) else 0) * 4 + iy)
            if slot is None:
                continue
            row = (0, xl, 1 - xl, 1)[ix] * CHIP
            if not isinstance(row, int):
                row = pl.multiple_of(row, CHIP)
            slots[slot, pl.ds(row, PART)] = pieces[last][0][inner]
            slots[slot, pl.ds(row + PART, PART)] = pieces[last][1][inner]


def place_both(pos_ref, own, other, x_place, xs, s_place, ss):
    @pl.when(pos_ref[2] == 0)
    def _():
        place_rows(pos_ref, own, True, x_place, xs)
        place_rows(pos_ref, other, False, s_place, ss)

    @pl.when(pos_ref[2] == 1)
    def _():
        place_rows(pos_ref, other, True, x_place, xs)
        place_rows(pos_ref, own, False, s_place, ss)


def columns_of(pos_ref, parity, iy):
    xl, y = pos_ref[0], pos_ref[1]
    offset = jnp.where(iy == 1, 1, jnp.where(iy == 2, 3, jnp.where(iy == 3, 2, 0)))
    block = ((xl + parity) % 2) * 4 + (y + offset) % 4
    return pl.ds(pl.multiple_of(block * SHARE, SHARE), SHARE)


LAST_DIMS = (((1,), (1,)), ((), ()))


def accumulate(pos_ref, acc, w_in, w_out, xs, ss, x_slots, s_slots):
    def x_step(t, carry):
        acc[: 2 * HID] += lax.dot_general(
            w_in[:, columns_of(pos_ref, *x_slots[1](t))],
            xs[t],
            LAST_DIMS,
            preferred_element_type=F32,
        )
        return carry

    def s_step(t, carry):
        acc[2 * HID :] += lax.dot_general(
            w_out[:, columns_of(pos_ref, *s_slots[1](t))],
            ss[t],
            LAST_DIMS,
            preferred_element_type=F32,
        )
        return carry

    lax.fori_loop(0, x_slots[0], x_step, 0)
    lax.fori_loop(0, s_slots[0], s_step, 0)


def early_kernel(pos_ref, w_in, w_out, *refs):
    own, other = [tuple(zip(refs[i : i + 3], refs[i + 3 : i + 6])) for i in (0, 6)]
    acc, xs, ss, token_ref = refs[-4:]
    token_ref[...] = jnp.zeros_like(token_ref)
    place_both(
        pos_ref, own, other,
        lambda j: (j // 4) * 3 + j % 4 if j % 4 < 3 else None, xs,
        lambda j: j - 4 if j >= 4 else None, ss,
    )
    acc[...] = jnp.zeros_like(acc)
    accumulate(
        pos_ref, acc, w_in, w_out, xs, ss,
        (6, lambda t: (t // 3, t % 3)), (4, lambda t: (1, t)),
    )


def late_kernel(pos_ref, w_in, w_out, early_ref, *refs):
    own, other = [
        (refs[i : i + 2], None, None, (refs[i + 2].at[0], refs[i + 2].at[1])) for i in (0, 3)
    ]
    xs, ss, d_ref, h_ref = refs[6:10]
    rows, scores, (acc, all_rows, score_ref) = refs[10:12], refs[12:14], refs[14:]
    place_both(
        pos_ref, own, other,
        lambda j: j // 4 if j % 4 == 3 else None, xs,
        lambda j: j if j < 4 else None, ss,
    )
    acc[...] = early_ref[...]
    accumulate(
        pos_ref, acc, w_in, w_out, xs, ss, (2, lambda t: (t, 3)), (4, lambda t: (0, t))
    )
    pre_gate, pre_up, back = acc[:HID], acc[HID : 2 * HID], acc[2 * HID :]
    tanh_part = jnp.tanh(
        SQRT_TWO_PI * (pre_gate + CUBIC * pre_gate * pre_gate * pre_gate)
    )
    gelu = 0.5 * pre_gate * (1.0 + tanh_part)
    slope = 0.5 * (1.0 + tanh_part) + 0.5 * pre_gate * (
        1.0 - tanh_part * tanh_part
    ) * SQRT_TWO_PI * (1.0 + 3.0 * CUBIC * pre_gate * pre_gate)
    hidden = (gelu * pre_up).astype(BF16)
    h_ref[...] = hidden
    score = jnp.sum(hidden.astype(F32) * back, axis=0, keepdims=True)
    score = jnp.broadcast_to(score, (8, ROWS))
    for b, start in enumerate((0, BLOCK, CHIP, CHIP + BLOCK)):
        turned = score if b == 0 else pltpu.roll(score, ROWS - start, 1)
        score_ref[b] = turned
    d_gate = back * pre_up * slope
    d_up = back * gelu
    d_ref[:HID] = d_gate.astype(BF16)
    d_ref[HID:] = d_up.astype(BF16)
    all_rows[...] = jnp.concatenate([d_gate, d_up], axis=0).T.astype(BF16)
    for i, core in enumerate((pos_ref[2], 1 - pos_ref[2])):
        for b in range(4):
            rows[i][b * BLOCK : (b + 1) * BLOCK] = all_rows[
                pl.ds(pl.multiple_of((2 * b + core) * BLOCK, BLOCK), BLOCK)
            ]
        for x_half in range(2):
            scores[i][x_half] = score_ref[2 * x_half + core]


def rows_kernel(pos_ref, w_own, w_pair, own_rows, pair_rows, own_score, pair_score, out):
    xl, core = pos_ref[0], pos_ref[2]

    def step(j, carry):
        parity, iy = j // 4, j % 4
        columns = columns_of(pos_ref, parity, iy)
        value = jnp.dot(own_rows[...], w_own[:, columns], preferred_element_type=F32)
        value += jnp.dot(pair_rows[...], w_pair[:, columns], preferred_element_type=F32)
        value = value.astype(BF16)
        for x_half in range(2):
            ix = jnp.where(parity == 0, 3 * x_half, 1 + (x_half + xl) % 2)
            first, second = jnp.where(core == 0, ix, iy), jnp.where(core == 0, iy, ix)
            out[first, second, 0:PART] = value[x_half * PART : (x_half + 1) * PART]
            out[first, second, PART:TALL] = (
                own_score[x_half] + pair_score[x_half]
            ).astype(BF16)
        return carry

    lax.fori_loop(0, 8, step, 0)


def weights_kernel(outputs, slots, skip, *refs):
    pos_ref, d_ref, arrays = refs[0], refs[1], refs[2:4]
    refs = refs[4 + skip :]
    outs, token_ref, gs, g_sem = refs[:outputs], *refs[outputs:]
    token_ref[...] = jnp.zeros_like(token_ref)
    done = 0
    for array, (count, features) in zip(arrays, slots):

        def copies(t):
            columns = columns_of(pos_ref, *features(t))
            return [
                pltpu.make_async_copy(
                    gs.at[done + t, pl.ds(i * HID, HID)],
                    outs[i].at[:, columns],
                    g_sem.at[done + t, i],
                )
                for i in range(outputs)
            ]

        def step(t, carry):
            gs[done + t] = jnp.dot(
                d_ref[...], array[t], preferred_element_type=F32
            ).astype(BF16)
            for copy in copies(t):
                copy.start()
            return carry

        lax.fori_loop(0, count, step, 0)
        done += count

    def drain(t, carry):
        for i in range(outputs):
            part = gs.at[t, pl.ds(i * HID, HID)]
            pltpu.make_async_copy(part, part, g_sem.at[t, i]).wait()
        return carry

    lax.fori_loop(0, 8, drain, 0)


def relay_kernel(token, part1, arrival1, part2, arrival2, out1, out2, token_ref):
    del token
    token_ref[...] = jnp.zeros_like(token_ref)
    for t in range(2):
        out1[t] = (part1[t].astype(F32) + arrival1[t].astype(F32)).astype(BF16)
        out2[t] = (part2[t].astype(F32) + arrival2[t].astype(F32)).astype(BF16)


def sum_kernel(token, own, next0, next1, prev0, prev1, *outs):
    del token
    for i, out in enumerate(outs):
        total = own[i].astype(F32)
        total = total + (next0, next1)[i // 2][i % 2].astype(F32)
        total = total + (prev0, prev1)[i // 2][i % 2].astype(F32)
        out[...] = total.astype(BF16)


def homes_kernel(*refs):
    parts, outs = refs[:4], refs[4:6]
    total = (
        parts[0][...].astype(F32)
        + parts[1][...].astype(F32)
        + parts[2][...].astype(F32)
        + parts[3][...].astype(F32)
    )
    scores = total[PART:TALL]
    for z, out in enumerate(outs):
        out[0:BLOCK] = total[z * BLOCK : (z + 1) * BLOCK].astype(BF16)
        if z == 1:
            scores = pltpu.roll(scores, SHARE - PART, 1)
        out[BLOCK : BLOCK + 8] = scores.astype(BF16)


def split_kernel(a_ref, b_ref, *outs):
    total = a_ref[...].astype(F32) + b_ref[...].astype(F32)
    for k, out in enumerate(outs):
        out[0:CAP] = total[k * CAP : (k + 1) * CAP].astype(BF16)
        out[CAP : CAP + 8] = total[BLOCK : BLOCK + 8].astype(BF16)


def pass_kernel(*refs):
    for z in range(2):
        for t in range(4):
            refs[5][z, t] = refs[1 + 2 * z + t // 2][t % 2]


SMEM = pl.BlockSpec(memory_space=pltpu.SMEM)
VMEM = pl.BlockSpec(memory_space=pltpu.VMEM)
ANY = pl.BlockSpec(memory_space=pl.ANY)
HBM = pl.BlockSpec(memory_space=pltpu.HBM)
DMA = pltpu.SemaphoreType.DMA


def shape(dims, dtype=BF16):
    return jax.ShapeDtypeStruct(dims, dtype)


def params(mib):
    return pltpu.CompilerParams(vmem_limit_bytes=mib * 1024 * 1024)


def cost(products, size):
    return pl.CostEstimate(flops=2 * products, bytes_accessed=size, transcendentals=0)


TOKEN = shape((8, 128), F32)


def weights_call(outputs, slots, pos, d, arrays, after):
    return pl.pallas_call(
        functools.partial(weights_kernel, outputs, slots, len(after)),
        out_shape=[shape((HID, WIDTH))] * outputs + [TOKEN],
        in_specs=[SMEM] + [VMEM] * 3 + [ANY] * len(after),
        out_specs=[ANY] * outputs + [VMEM],
        scratch_shapes=[
            pltpu.VMEM((8, outputs * HID, SHARE), BF16),
            DMA((8, outputs)),
        ],
        compiler_params=params(6),
        cost_estimate=cost(
            outputs * HID * ROWS * WIDTH, 2 * WIDTH * (ROWS + outputs * HID)
        ),
    )(pos, d, *arrays, *after)


def scatter(parts, first):
    return [cross(parts[i], first, -OFFSET[i]) for i in (3, 1, 2)] + [parts[0]]


def between(value, k, dz):
    pairs = [
        ((((e + k) % 4) * 2 + (z ^ dz)), e * 2 + z) for e in range(4) for z in range(2)
    ]
    return lax.ppermute(value, ("e", "zl"), pairs)


def body(tokens, grad_out, expert_ids, slot_ids, gate_weights, gate_proj, up_proj, down_proj):
    core = lax.axis_index("c")
    pos = jnp.stack([lax.axis_index("xl"), lax.axis_index("y"), core]).astype(jnp.int32)
    relative = (expert_ids.T - lax.axis_index("e") + EXPERTS) % EXPERTS
    target = jnp.where(slot_ids.T >= 0, relative * CAP + slot_ids.T, -1)
    info = jnp.concatenate([target.astype(BF16), gate_weights.T], axis=0)
    keep = jnp.where(core == 0, tokens, grad_out)
    give = jnp.where(core == 0, grad_out, tokens)
    packed = pl.pallas_call(
        pack_kernel,
        out_shape=[shape((2 * CAP, SHARE))] * EXPERTS,
        in_specs=[SMEM] + [VMEM] * 4,
        out_specs=[VMEM] * EXPERTS,
        compiler_params=params(2),
    )(pos, info, fetch(info, "c", 1, 2), keep, fetch(give, "c", 1, 2))
    arrived = [between(packed[k], -k, 0) for k in ORDER[:3]] + [packed[0]]
    mine = pl.pallas_call(
        order_kernel,
        out_shape=shape((2, BLOCK, SHARE)),
        in_specs=[VMEM] * EXPERTS,
        out_specs=VMEM,
        compiler_params=params(2),
    )(*arrived)
    theirs = fetch(mine, "zl", 1, 2)
    group, stacks = [cross(mine, True, d) for d in (2, 1, -1)] + [mine], []
    for z in range(2):
        after = () if z else (theirs,)
        stacked, token = pl.pallas_call(
            stack_kernel,
            out_shape=[shape((4, PART, SHARE)), TOKEN],
            in_specs=[VMEM] * 4 + [ANY] * len(after),
            out_specs=[VMEM] * 2,
            compiler_params=params(4),
        )(*group, *after)
        stacks.append(stacked)
        theirs = pl.pallas_call(
            copy_kernel,
            out_shape=shape((2, BLOCK, SHARE)),
            in_specs=[VMEM, ANY],
            out_specs=VMEM,
            compiler_params=params(2),
        )(theirs, group[0])
        if not z:
            group = [cross(theirs, True, d) for d in (2, 1, -1)] + [theirs]
    w_in, w_out = pl.pallas_call(
        join_kernel,
        out_shape=[shape((2 * HID, WIDTH)), shape((HID, WIDTH))],
        in_specs=[VMEM] + [HBM] * 3,
        out_specs=[VMEM] * 2,
        scratch_shapes=[DMA((3,))],
        compiler_params=params(2),
        cost_estimate=cost(0, 12 * HID * WIDTH),
    )(token, gate_proj[0], up_proj[0], down_proj[0])
    w_pair = fetch(w_in, "c", 1, 2)
    own, halves = [], []
    for t in stacks:
        nxt, prev = cross(t, False, 1), cross(t, False, -1)
        own += [t, nxt, prev]
        halves += [cross(prev[:2], False, -1), cross(nxt[2:], False, 1)]
    other = [fetch(t, "c", 1, 2) for t in own]
    early, xs_early, ss_early, token = pl.pallas_call(
        early_kernel,
        out_shape=[
            shape((3 * HID, ROWS), F32),
            shape((6, ROWS, SHARE)),
            shape((4, ROWS, SHARE)),
            TOKEN,
        ],
        in_specs=[SMEM] + [VMEM] * 14,
        out_specs=[VMEM] * 4,
        compiler_params=params(4),
        cost_estimate=cost(0, 0),
    )(pos, w_in, w_out, *own, *other)
    last = pl.pallas_call(
        pass_kernel,
        out_shape=shape((2, 4, PART, SHARE)),
        in_specs=[ANY] + [VMEM] * 4,
        out_specs=VMEM,
        compiler_params=params(4),
    )(token, *halves)
    half_rows, half_score = shape((ROWS // 2, 2 * HID)), shape((2, 8, ROWS), F32)
    xs_late, ss_late, d, hidden, rows, pair_rows, score, pair_score = pl.pallas_call(
        late_kernel,
        out_shape=[
            shape((2, ROWS, SHARE)),
            shape((4, ROWS, SHARE)),
            shape((2 * HID, ROWS)),
            shape((HID, ROWS)),
            half_rows,
            half_rows,
            half_score,
            half_score,
        ],
        in_specs=[SMEM] + [VMEM] * 9,
        out_specs=[VMEM] * 8,
        scratch_shapes=[
            pltpu.VMEM((3 * HID, ROWS), F32),
            pltpu.VMEM((ROWS, 2 * HID), BF16),
            pltpu.VMEM((4, 8, ROWS), F32),
        ],
        compiler_params=params(10),
        cost_estimate=cost(
            HID * ROWS * WIDTH, 2 * WIDTH * (3 * HID + ROWS * 3 // 4)
        ),
    )(
        pos, w_in, w_out, early, *stacks, last, other[0], other[3], fetch(last, "c", 1, 2)
    )
    sums = pl.pallas_call(
        rows_kernel,
        out_shape=shape((4, 4, TALL, SHARE)),
        in_specs=[SMEM] + [VMEM] * 6,
        out_specs=VMEM,
        compiler_params=params(4),
        cost_estimate=cost(
            2 * HID * ROWS * WIDTH, 2 * WIDTH * (ROWS // 2 + 4 * HID)
        ),
    )(
        pos, w_in, w_pair, rows, fetch(pair_rows, "c", 1, 2), score, fetch(pair_score, "c", 1, 2)
    )
    part = sums[0]
    halves = [[sums[i, t : t + 2] for t in (0, 2)] for i in range(1, 4)]
    arrivals = [cross(halves[2][0], True, -1), cross(halves[2][1], True, 1)]
    from_prev, from_next = cross(halves[0][1], True, -1), cross(halves[1][0], True, 1)
    grad_down, token = weights_call(
        1, ((4, lambda t: (1, t)), (4, lambda t: (0, t))), pos, hidden, (ss_early, ss_late),
        (halves[2][0],),
    )
    to_next, to_prev, token = pl.pallas_call(
        relay_kernel,
        out_shape=[shape((2, TALL, SHARE))] * 2 + [TOKEN],
        in_specs=[ANY] + [VMEM] * 4,
        out_specs=[VMEM] * 3,
        compiler_params=params(4),
    )(token, halves[0][0], arrivals[0], halves[1][1], arrivals[1])
    grad_gate, grad_up, token = weights_call(
        2, ((6, lambda t: (t // 3, t % 3)), (2, lambda t: (t, 3))), pos, d, (xs_early, xs_late),
        (token,),
    )
    parts = pl.pallas_call(
        sum_kernel,
        out_shape=[shape((TALL, SHARE))] * 4,
        in_specs=[ANY] + [VMEM] * 5,
        out_specs=[VMEM] * 4,
        compiler_params=params(4),
    )(
        token, part, cross(to_next, True, -1), from_prev, from_next, cross(to_prev, True, 1)
    )
    here, there = pl.pallas_call(
        homes_kernel,
        out_shape=[shape((BLOCK + 8, SHARE))] * 2,
        in_specs=[VMEM] * 4,
        out_specs=[VMEM] * 2,
        compiler_params=params(4),
    )(*scatter(parts, False))
    blocks = pl.pallas_call(
        split_kernel,
        out_shape=[shape((CAP + 8, SHARE))] * EXPERTS,
        in_specs=[VMEM] * 2,
        out_specs=[VMEM] * EXPERTS,
        compiler_params=params(4),
    )(here, fetch(there, "zl", 1, 2))
    blocks = [between(blocks[k], k, 0) for k in ORDER[:3]] + [blocks[0]]

    grad_tokens, grad_gates = pl.pallas_call(
        combine_kernel,
        out_shape=[shape((TOK, SHARE)), shape((2, TOK), F32)],
        in_specs=[VMEM] * 5,
        out_specs=[VMEM] * 2,
        compiler_params=params(4),
    )(info, *blocks)
    return (grad_tokens, grad_gates.T, grad_gate[None], grad_up[None], grad_down[None])


def solution(mesh):
    parts = Mesh(
        mesh.devices.reshape(4, 2, 2, 2, 2, 4), ("e", "zl", "xh", "c", "xl", "y")
    )
    ex, mp = ("e", "zl", "xh", "c"), ("xl", "y")
    return jax.shard_map(
        body,
        mesh=parts,
        in_specs=(
            P(ex, mp),
            P(ex, mp),
            P(ex, None),
            P(ex, None),
            P(ex, None),
            P(ex, mp, None),
            P(ex, mp, None),
            P(ex, mp, None),
        ),
        out_specs=(
            P(ex, mp),
            P(ex, None),
            P(ex, mp, None),
            P(ex, mp, None),
            P(ex, mp, None),
        ),
        check_vma=False,
    )
```
